512 devices in a mesh: ctx: 64 (over y, z), tp: 8 (over x, core).
Axes of the slice: x: 4, y: 4, z: 16, core: 2. Of those that a mesh axis runs over, the one named last changes fastest.
Arguments:
- grad_out: bfloat16 [8192, 4096], P('ctx', 'tp'), may hold values from -6 to 6
- gate: bfloat16 [8192, 4096], P('ctx', 'tp'), may hold values from -6 to 6
- conv_input: bfloat16 [8192, 4096], P('ctx', 'tp'), may hold values from -6 to 6
- out_weight: bfloat16 [4096, 4096], P('tp', 'ctx'), may hold values from -0.09375 to 0.09375
- residues: float32 [16, 4096], P(None, 'tp'), may hold values from -0.12 to 0.12
- rates: float32 [16, 4096], P(None, 'tp'), may hold values from 6.1035156e-05 to 0.04
Outputs:
- input_grad: bfloat16 [8192, 4096], P('ctx', 'tp')
- residue_grad: float32 [16, 4096], P(None, 'tp')
The draws below stay inside these ranges and needn't reach their ends.
All inputs are finite; a program needn't handle non-finite values.
Results may differ from the reference program's by a relative error of at most 0.0027.
Values may be sent and summed in bfloat16 or wider, within the bound.
A program may use at most 64 MiB of HBM per device.

```python
import math
import jax
import jax.numpy as jnp
from jax import lax

D = 4096
MODES = 16
LENGTH = 8192


def levels(rng, dims, pieces, smallest, top_value):
    def one(position, shards_of):
        heights = jax.random.uniform(jax.random.fold_in(jax.random.fold_in(rng, 6), position), (shards_of,), jnp.float32, smallest / len(pieces), top_value / len(pieces))
        return jnp.repeat(jnp.exp(heights), dims[position] // shards_of).reshape((-1,) + (1,) * (len(dims) - position - 1))

    level = one(*pieces[0])
    for cut in pieces[1:]:
        level = level * one(*cut)
    return level


def bell_draw(stream_key, dims, deviation, bound, pieces=(), kind=jnp.bfloat16):
    result = deviation * jax.random.normal(stream_key, dims, jnp.float32)
    if pieces:
        result = result * levels(stream_key, dims, pieces, -0.22, 0.18)
    return jnp.clip(result, -bound, bound).astype(kind)


def setup_inputs(seed: int = 0) -> dict:
    splits = jax.random.split(jax.random.key(seed), 7)
    grad_out = bell_draw(splits[0], (LENGTH, D), 1.0, 6.0, ((0, 64), (1, 8)))
    gate = bell_draw(splits[1], (LENGTH, D), 1.0, 6.0, ((0, 64), (1, 8)))
    conv_input = bell_draw(splits[2], (LENGTH, D), 1.0, 6.0, ((0, 64), (1, 8)))
    out_weight = bell_draw(splits[3], (D, D), D ** -0.5, 0.09375, ((0, 8), (1, 64)))
    residues = bell_draw(splits[4], (MODES, D), 0.02, 0.12, ((1, 8),), jnp.float32)
    rates = jnp.clip(jnp.exp(math.log(0.04) - 6.4851847 * jax.random.uniform(splits[5], (MODES, D), jnp.float32) ** levels(splits[5], (MODES, D), ((1, 8),), -0.2, 0.2)), 6.103515625e-05, 0.04)
    return {"grad_out": grad_out, "gate": gate, "conv_input": conv_input, "out_weight": out_weight, "residues": residues, "rates": rates}


def reference(grad_out, gate, conv_input, out_weight, residues, rates):
    grad_y = jnp.dot(grad_out, out_weight.T, preferred_element_type=jnp.float32)
    grad_conv = gate.astype(jnp.float32) * grad_y
    values = conv_input.astype(jnp.float32)
    decay = jnp.exp(-rates)

    def step(carry, row):
        state, total = carry
        grad_row, value_row = row
        state = decay * state + grad_row[None, :]
        total = total + value_row[None, :] * state
        return (state, total), jnp.sum(residues * state, axis=0)

    start = (jnp.zeros((MODES, D), jnp.float32), jnp.zeros((MODES, D), jnp.float32))
    (_, total), out_rows = lax.scan(step, start, (grad_conv, values), reverse=True)
    return out_rows.astype(jnp.bfloat16), total / jnp.float32(LENGTH)
```

```python
import jax
import jax.numpy as jnp
from jax import lax
from jax.experimental import pallas as pl
from jax.experimental.pallas import tpu as pltpu
from jax.sharding import PartitionSpec as P

MESH = pl.DeviceIdType.MESH
F32 = jnp.float32
BF16 = jnp.bfloat16
MODES = 16
NX = 4
NY = 4
NZ = 16
ROWS = 128
WIDE = 512
LANES = 128
SEG = 64
LENGTH = 8192


def kernel(
    go, gate, conv, weight, residues, rates,
    out, rout,
    gobuf, wbuf, wt, gt, cv, rt, rs,
    dec, resb, gc, cvf, near, starts, arrived, ends, ends_in, backs, incoming, rowsum, rowsum_in,
    outf, outb, rcomp,
    loc_sem, wy_s, wy_r, go_s, go_r, sib_s, sib_r, gc_s, gc_r, z_s, z_r,
    a_s, a_r, e_s, e_r, b_s, b_r, t_s, t_r, o_s, o_r, ro_s, ro_r,
):
    ctx = lax.axis_index("ctx")
    tp = lax.axis_index("tp")
    x, k = tp // 2, tp % 2
    y, z = ctx // NZ, ctx % NZ
    xp, xm, x2 = (x + 1) % NX, (x + 3) % NX, (x + 2) % NX
    yp, ym, y2 = (y + 1) % NY, (y + 3) % NY, (y + 2) % NY
    zp, zm = (z + 1) % NZ, (z + NZ - 1) % NZ

    def dev(dx=None, dy=None, dz=None, dk=None):
        xx = x if dx is None else dx
        yy = y if dy is None else dy
        zz = z if dz is None else dz
        kk = k if dk is None else dk
        return (yy * NZ + zz, xx * 2 + kk)

    near_devices = [dev(dx=xp), dev(dx=xm), dev(dy=yp), dev(dy=ym), dev(dy=y2), dev(dz=zp), dev(dz=zm), dev(dk=1 - k)]
    barrier = pltpu.get_barrier_semaphore()
    for d in near_devices:
        pl.semaphore_signal(barrier, inc=1, device_id=d, device_id_type=MESH)

    unsent = []

    def send(src, dst, ss, rs_, target):
        c = pltpu.make_async_remote_copy(
            src_ref=src, dst_ref=dst, send_sem=ss, recv_sem=rs_, device_id=target, device_id_type=MESH
        )
        c.start()
        unsent.append(c)

    def wait_in(ref, sem):
        pltpu.make_async_copy(ref, ref, sem).wait()

    cols = pl.ds(pl.multiple_of(y * LANES, LANES), LANES)
    me = x * 2 + k
    locals_ = [
        pltpu.make_async_copy(go, gobuf.at[me, y], loc_sem.at[0]),
        pltpu.make_async_copy(gate.at[:, cols], gt.at[y], loc_sem.at[1]),
        pltpu.make_async_copy(conv.at[:, cols], cv.at[y], loc_sem.at[2]),
        pltpu.make_async_copy(rates.at[:, cols], rt, loc_sem.at[3]),
        pltpu.make_async_copy(residues.at[:, cols], rs, loc_sem.at[4]),
    ]
    for c in locals_:
        c.start()
    for q in range(NY):
        wt[q] = weight[q * LANES : (q + 1) * LANES, :].astype(F32).T.astype(BF16)
    wbuf[0, z] = wt[y]
    for c in locals_:
        c.wait()
    for m in range(MODES):
        dec[m] = jnp.broadcast_to(jnp.exp(-rt[m : m + 1, :]), (8, LANES))
        resb[m] = jnp.broadcast_to(rs[m : m + 1, :], (8, LANES))

    pl.semaphore_wait(barrier, len(near_devices))

    for r in range(1, NY):
        to = (y + NY - r) % NY
        send(wt.at[to], wbuf.at[r, z], wy_s.at[r], wy_r.at[r], dev(dy=to))

    A, B = (0, 64), (64, 64)
    A0, A1, B0, B1 = (0, 32), (32, 32), (64, 32), (96, 32)
    go_slots = {}

    def go_ref(ox, oy, piece):
        return gobuf.at[ox * 2 + k, oy, pl.ds(piece[0], piece[1]), :]

    def go_send(key, ox, oy, piece, target, src=None):
        slot = go_slots.setdefault(key, len(go_slots))
        ref = go_ref(ox, oy, piece)
        send(ref if src is None else src, ref, go_s.at[slot], go_r.at[slot], target)

    def go_wait(key, ox, oy, piece):
        wait_in(go_ref(ox, oy, piece), go_r.at[go_slots[key]])

    def own(piece):
        return go.at[pl.ds(piece[0], piece[1]), :]

    go_send(("+x", "L", "A"), x, y, A, dev(dx=xp), own(A))
    go_send(("-x", "R", "A"), x, y, A, dev(dx=xm), own(A))
    go_send(("+y", "D", "B"), x, y, B, dev(dy=yp), own(B))
    go_send(("-y", "U", "B"), x, y, B, dev(dy=ym), own(B))
    go_send(("+x", "L", "B"), x, y, B, dev(dx=xp), own(B))
    go_send(("-x", "R", "B"), x, y, B, dev(dx=xm), own(B))
    go_send(("+y", "D", "A"), x, y, A, dev(dy=yp), own(A))
    go_send(("-y", "U", "A"), x, y, A, dev(dy=ym), own(A))

    sib_slots = []

    def sibling(ox, oy, src=None):
        slot = len(sib_slots)
        ref = gobuf.at[ox * 2 + k, oy]
        send(ref if src is None else src, ref, sib_s.at[slot], sib_r.at[slot], dev(dk=1 - k))
        sib_slots.append((ox, oy))

    sibling(x, y, go)

    HALVES = (0, 2)

    def z_send(way, sub, step, owner, target):
        ref = wbuf.at[pl.ds(sub, 2), owner]
        i = (way * 2 + sub // 2) * 8 + step - 1
        send(ref, ref, z_s.at[i], z_r.at[i], target)

    def z_wait(way, sub, step, owner):
        i = (way * 2 + sub // 2) * 8 + step - 1
        wait_in(wbuf.at[pl.ds(sub, 2), owner], z_r.at[i])

    def z_start(sub):
        for r in (sub, sub + 1):
            if r:
                wait_in(wbuf.at[r, z], wy_r.at[r])
        z_send(0, sub, 1, z, dev(dz=zp))
        z_send(1, sub, 1, z, dev(dz=zm))

    def z_round(step):
        for sub in HALVES:
            for way in (0, 1):
                if step == 8 and way != sub // 2:
                    continue
                owner = (z + NZ - step) % NZ if way == 0 else (z + step) % NZ
                z_wait(way, sub, step, owner)
                if step < 7 or (step == 7 and way == sub // 2):
                    z_send(way, sub, step + 1, owner, dev(dz=zp) if way == 0 else dev(dz=zm))

    z_start(0)
    z_start(2)

    for r in range(1, NY):
        to = (y + r) % NY
        tc = pl.ds(pl.multiple_of(to * LANES, LANES), LANES)
        send(gate.at[:, tc], gt.at[y], gc_s.at[r], gc_r.at[r], dev(dy=to))
        send(conv.at[:, tc], cv.at[y], gc_s.at[4 + r], gc_r.at[4 + r], dev(dy=to))

    z_round(1)
    go_wait(("+x", "L", "A"), xm, y, A)
    go_send(("+x", "X2", "A"), xm, y, A, dev(dx=xp))
    go_send(("+y", "L,D", "A"), xm, y, A, dev(dy=yp))
    go_send(("-y", "L,U", "A"), xm, y, A, dev(dy=ym))
    go_wait(("-y", "U", "B"), x, yp, B)
    go_send(("-y", "Y2", "B"), x, yp, B, dev(dy=ym))
    go_send(("+x", "U,L", "B"), x, yp, B, dev(dx=xp))
    go_send(("-x", "U,R", "B"), x, yp, B, dev(dx=xm))
    go_wait(("-x", "R", "A"), xp, y, A)
    go_send(("+y", "R,D", "A"), xp, y, A, dev(dy=yp))
    go_send(("-y", "R,U", "A"), xp, y, A, dev(dy=ym))
    go_wait(("+y", "D", "B"), x, ym, B)
    go_send(("+x", "D,L", "B"), x, ym, B, dev(dx=xp))
    go_send(("-x", "D,R", "B"), x, ym, B, dev(dx=xm))
    z_round(2)
    go_wait(("-x", "R", "B"), xp, y, B)
    go_send(("-x", "X2", "B"), xp, y, B, dev(dx=xm))
    go_wait(("+y", "D", "A"), x, ym, A)
    go_send(("+y", "Y2", "A"), x, ym, A, dev(dy=yp))
    go_wait(("+x", "L", "B"), xm, y, B)
    go_wait(("-y", "U", "A"), x, yp, A)
    sibling(xm, y)
    sibling(xp, y)
    sibling(x, ym)
    sibling(x, yp)
    z_round(3)
    go_wait(("+x", "X2", "A"), x2, y, A)
    go_send(("+y", "X2,D", "A"), x2, y, A, dev(dy=yp))
    go_send(("-y", "X2,U", "A"), x2, y, A, dev(dy=ym))
    go_wait(("-y", "Y2", "B"), x, y2, B)
    go_send(("+x", "Y2,L", "B"), x, y2, B, dev(dx=xp))
    go_send(("-x", "Y2,R", "B"), x, y2, B, dev(dx=xm))
    z_round(4)
    for col, ox in (("L", xm), ("R", xp)):
        go_wait(("+y", col + ",D", "A"), ox, ym, A)
        go_send(("+y", col + ",Y2", "A0"), ox, ym, A0, dev(dy=yp))
        go_wait(("-y", col + ",U", "A"), ox, yp, A)
        go_send(("-y", col + ",Y2", "A1"), ox, yp, A1, dev(dy=ym))
    for row, oy in (("D", ym), ("U", yp)):
        go_wait(("+x", row + ",L", "B"), xm, oy, B)
        go_send(("+x", row + ",X2", "B0"), xm, oy, B0, dev(dx=xp))
        go_wait(("-x", row + ",R", "B"), xp, oy, B)
        go_send(("-x", row + ",X2", "B1"), xp, oy, B1, dev(dx=xm))
    for ox in (xm, xp):
        for oy in (ym, yp):
            sibling(ox, oy)
    z_round(5)
    go_wait(("-x", "X2", "B"), x2, y, B)
    go_wait(("+y", "Y2", "A"), x, y2, A)
    sibling(x2, y)
    sibling(x, y2)
    z_round(6)
    for r in range(1, NY):
        src = (y + NY - r) % NY
        wait_in(gt.at[src], gc_r.at[r])
        wait_in(cv.at[src], gc_r.at[4 + r])
    for q in range(NY):
        cvf[q * ROWS : (q + 1) * ROWS, :] = cv[q].astype(F32)

    def end_step(t, sums):
        c = cvf[pl.ds(t, 8, stride=SEG), :]
        return tuple(dec[m] * (s + c) for m, s in enumerate(sums))

    zeros = tuple(jnp.zeros((8, LANES), F32) for _ in range(MODES))
    for m, s in enumerate(lax.fori_loop(0, SEG, end_step, zeros)):
        ends[m, 0] = s
    go_wait(("+y", "X2,D", "A"), x2, ym, A)
    go_send(("+y", "X2,Y2", "A0"), x2, ym, A0, dev(dy=yp))
    go_wait(("-y", "X2,U", "A"), x2, yp, A)
    go_send(("-y", "X2,Y2", "A1"), x2, yp, A1, dev(dy=ym))
    go_wait(("+x", "Y2,L", "B"), xm, y2, B)
    go_send(("+x", "Y2,X2", "B0"), xm, y2, B0, dev(dx=xp))
    go_wait(("-x", "Y2,R", "B"), xp, y2, B)
    go_send(("-x", "Y2,X2", "B1"), xp, y2, B1, dev(dx=xm))
    z_round(7)
    for col, ox in (("L", xm), ("R", xp)):
        go_wait(("+y", col + ",Y2", "A0"), ox, y2, A0)
        go_wait(("-y", col + ",Y2", "A1"), ox, y2, A1)
        sibling(ox, y2)
    for row, oy in (("D", ym), ("U", yp)):
        go_wait(("+x", row + ",X2", "B0"), x2, oy, B0)
        go_wait(("-x", row + ",X2", "B1"), x2, oy, B1)
        sibling(x2, oy)
    z_round(8)
    go_wait(("+y", "X2,Y2", "A0"), x2, y2, A0)
    go_wait(("-y", "X2,Y2", "A1"), x2, y2, A1)
    go_wait(("+x", "Y2,X2", "B0"), x2, y2, B0)
    go_wait(("-x", "Y2,X2", "B1"), x2, y2, B1)
    sibling(x2, y2)
    for slot, (ox, oy) in enumerate(sib_slots):
        wait_in(gobuf.at[ox * 2 + 1 - k, oy], sib_r.at[slot])

    total = jnp.zeros((NY * ROWS, LANES), F32)
    for ox in range(NX):
        rel = (ox + NY - y) % NY
        for half in range(2):
            a = gobuf[ox * 2 + half].reshape(NY * ROWS, WIDE)
            w = wbuf[rel, half * 8 : half * 8 + 8].reshape(WIDE, LANES)
            total = total + jnp.dot(a, w, preferred_element_type=F32)
    gc[...] = total * gt[...].reshape(NY * ROWS, LANES).astype(F32)

    def start_step(i, sums):
        g = gc[pl.ds(SEG - 1 - i, 8, stride=SEG), :]
        return tuple(dec[m] * s + g for m, s in enumerate(sums))

    for m, s in enumerate(lax.fori_loop(0, SEG, start_step, zeros)):
        starts[m] = s

    def far_first():
        order = [8]
        for d in range(7, 0, -1):
            order += [d, NZ - d]
        return order

    arrived[z] = starts[z]
    for d in far_first():
        to = (z + d) % NZ
        send(starts.at[to], arrived.at[z], a_s.at[d], a_r.at[d], dev(dz=to))

    def near_step(i, carry):
        sums, inner = carry
        t = SEG - 1 - i
        g = gc[pl.ds(t, 8, stride=SEG), :]
        c = cvf[pl.ds(t, 8, stride=SEG), :]
        sums = tuple(dec[m] * s + g for m, s in enumerate(sums))
        inner = tuple(n + c * s for n, s in zip(inner, sums))
        acc = resb[0] * sums[0]
        for m in range(1, MODES):
            acc = acc + resb[m] * sums[m]
        near[t] = acc
        return sums, inner

    _, inner = lax.fori_loop(0, SEG, near_step, (zeros, zeros))
    for m in range(MODES):
        ends[m, 1] = inner[m]
    ends_in[z] = ends[z]
    for d in far_first():
        to = (z + d) % NZ
        send(ends.at[to], ends_in.at[z], e_s.at[d], e_r.at[d], dev(dz=to))

    for d in range(1, NZ):
        wait_in(arrived.at[(z + NZ - d) % NZ], a_r.at[d])
    rate = jnp.broadcast_to(rt[pl.ds(z, 1), :], (8, LANES))
    row = lax.broadcasted_iota(jnp.int32, (8, LANES), 0)
    even = row % 2 == 0
    by_seg = jnp.exp(-rate * F32(SEG))
    by_block = jnp.exp(-rate * F32(ROWS))
    by_line = jnp.exp(-rate * F32(ROWS * NZ))
    second, block = [], []
    for zz in range(NZ):
        s = arrived[zz]
        other = jnp.where(even, pltpu.roll(s, 7, 0), pltpu.roll(s, 1, 0))
        first = jnp.where(even, s, other)
        second.append(jnp.where(even, other, s))
        block.append(first + by_seg * second[zz])
    after = [None] * NZ
    after[NZ - 1] = jnp.zeros((8, LANES), F32)
    for zz in range(NZ - 2, -1, -1):
        after[zz] = block[zz + 1] + by_block * after[zz + 1]
    line = block[0] + by_block * after[0]

    def next_row(v):
        return jnp.where(row < 6, pltpu.roll(v, 6, 0), 0.0)

    line_next = next_row(line)
    lines = line_next
    for _ in range(2):
        lines = line_next + by_line * next_row(lines)
    ins = []
    for zz in range(NZ):
        late = after[zz] + jnp.exp(-rate * F32(ROWS * (NZ - 1 - zz))) * lines
        ins.append(jnp.where(even, second[zz] + by_seg * late, late))
        backs[zz] = ins[zz]
    incoming[z] = backs[z]
    for d in far_first():
        to = (z + d) % NZ
        send(backs.at[to], incoming.at[z], b_s.at[d], b_r.at[d], dev(dz=to))

    for d in range(1, NZ):
        wait_in(ends_in.at[(z + NZ - d) % NZ], e_r.at[d])
    grad = jnp.zeros((8, LANES), F32)
    for zz in range(NZ):
        grad = grad + (ends_in[zz, 1] + ends_in[zz, 0] * ins[zz])
    rowsum[...] = jnp.sum(grad, axis=0, keepdims=True) * F32(1.0 / LENGTH)
    rowsum_in[z] = rowsum[...]
    for d in far_first():
        to = (z + d) % NZ
        send(rowsum, rowsum_in.at[z], t_s.at[d], t_r.at[d], dev(dz=to))

    for d in range(1, NZ):
        wait_in(incoming.at[(z + NZ - d) % NZ], b_r.at[d])

    def far_step(i, sums):
        t = SEG - 1 - i
        sums = tuple(dec[m] * s for m, s in enumerate(sums))
        acc = near[t]
        for m in range(MODES):
            acc = acc + resb[m] * sums[m]
        outf[pl.ds(t, 8, stride=SEG), :] = acc
        return sums

    lax.fori_loop(0, SEG, far_step, tuple(incoming[m] for m in range(MODES)))
    for q in range(NY):
        outb[q] = outf[q * ROWS : (q + 1) * ROWS, :].astype(BF16)
    for r in (2, 1, 3):
        to = (y + r) % NY
        send(outb.at[to], out.at[:, cols], o_s.at[r], o_r.at[r], dev(dy=to))
    out[:, cols] = outb[y]

    for d in range(1, NZ):
        wait_in(rowsum_in.at[(z + NZ - d) % NZ], t_r.at[d])
    for m in range(MODES):
        rcomp[m : m + 1, :] = rowsum_in[m]
    for r in (2, 1, 3):
        to = (y + r) % NY
        send(rcomp, rout.at[:, cols], ro_s.at[r], ro_r.at[r], dev(dy=to))
    rout[:, cols] = rcomp[...]
    for r in range(1, NY):
        src = pl.ds(pl.multiple_of(((y + NY - r) % NY) * LANES, LANES), LANES)
        wait_in(out.at[:, src], o_r.at[r])
        wait_in(rout.at[:, src], ro_r.at[r])
    for c in unsent:
        c.wait_send()


def local(grad_out, gate, conv_input, out_weight, residues, rates):
    any_ = pl.BlockSpec(memory_space=pl.ANY)
    vmem = pl.BlockSpec(memory_space=pltpu.VMEM)
    dma = pltpu.SemaphoreType.DMA
    return pl.pallas_call(
        kernel,
        name="modal_backward",
        out_shape=(
            jax.ShapeDtypeStruct((ROWS, WIDE), BF16),
            jax.ShapeDtypeStruct((MODES, WIDE), F32),
        ),
        in_specs=[any_, any_, any_, vmem, any_, any_],
        out_specs=(vmem, vmem),
        scratch_shapes=[
            pltpu.VMEM((2 * NX, NY, ROWS, WIDE), BF16),
            pltpu.VMEM((NY, NZ, 64, LANES), BF16),
            pltpu.VMEM((NY, 64, LANES), BF16),
            pltpu.VMEM((NY, ROWS, LANES), BF16),
            pltpu.VMEM((NY, ROWS, LANES), BF16),
            pltpu.VMEM((MODES, LANES), F32),
            pltpu.VMEM((MODES, LANES), F32),
            pltpu.VMEM((MODES, 8, LANES), F32),
            pltpu.VMEM((MODES, 8, LANES), F32),
            pltpu.VMEM((NY * ROWS, LANES), F32),
            pltpu.VMEM((NY * ROWS, LANES), F32),
            pltpu.VMEM((SEG, 8, LANES), F32),
            pltpu.VMEM((MODES, 8, LANES), F32),
            pltpu.VMEM((NZ, 8, LANES), F32),
            pltpu.VMEM((MODES, 2, 8, LANES), F32),
            pltpu.VMEM((NZ, 2, 8, LANES), F32),
            pltpu.VMEM((NZ, 8, LANES), F32),
            pltpu.VMEM((MODES, 8, LANES), F32),
            pltpu.VMEM((1, LANES), F32),
            pltpu.VMEM((MODES, 1, LANES), F32),
            pltpu.VMEM((NY * ROWS, LANES), F32),
            pltpu.VMEM((NY, ROWS, LANES), BF16),
            pltpu.VMEM((MODES, LANES), F32),
            dma((5,)),
            dma((4,)), dma((4,)),
            dma((36,)), dma((36,)),
            dma((16,)), dma((16,)),
            dma((8,)), dma((8,)),
            dma((32,)), dma((32,)),
            dma((16,)), dma((16,)),
            dma((16,)), dma((16,)),
            dma((16,)), dma((16,)),
            dma((16,)), dma((16,)),
            dma((4,)), dma((4,)),
            dma((4,)), dma((4,)),
        ],
        compiler_params=pltpu.CompilerParams(
            collective_id=1, has_side_effects=True, vmem_limit_bytes=32 << 20
        ),
    )(grad_out, gate, conv_input, out_weight, residues, rates)


def solution(mesh):
    placed = (
        P("ctx", "tp"),
        P("ctx", "tp"),
        P("ctx", "tp"),
        P("tp", "ctx"),
        P(None, "tp"),
        P(None, "tp"),
    )
    return jax.shard_map(
        local,
        mesh=mesh,
        in_specs=placed,
        out_specs=(P("ctx", "tp"), P(None, "tp")),
        check_vma=False,
    )
```

```python
import jax
import jax.numpy as jnp
from jax import lax
from jax.experimental import pallas as pl
from jax.experimental.pallas import tpu as pltpu
from jax.sharding import PartitionSpec as P

MESH = pl.DeviceIdType.MESH
F32 = jnp.float32
BF16 = jnp.bfloat16
MODES = 16
NX = 4
NY = 4
NZ = 16
ROWS = 128
WIDE = 512
LANES = 128
SEG = 64
LENGTH = 8192


def kernel(
    go, gate, conv, weight, residues, rates,
    out, rout,
    gobuf, wbuf, gtcv, rt, rs, rt_all, rs_all,
    dec, resb, dec_all, resb_all, gc, cvf, nearf, near, starts, ends, sent, arrived, sent_end, arrived_end,
    inrow, inrow_in, backs, incoming, rowsum, rowsum_in, outf,
    loc_sem, go_s, go_r, sib_r, z_s, z_r, gc_s, gc_r,
    a_s, a_r, e_s, e_r, i_s, i_r, n_s, n_r, b_s, b_r, t_s, t_r,
):
    ctx = lax.axis_index("ctx")
    tp = lax.axis_index("tp")
    x, k = tp // 2, tp % 2
    y, z = ctx // NZ, ctx % NZ
    xp, xm, x2 = (x + 1) % NX, (x + 3) % NX, (x + 2) % NX
    yp, ym, y2 = (y + 1) % NY, (y + 3) % NY, (y + 2) % NY

    def up(n):
        return (z + NZ + n) % NZ

    def dev(dx=None, dy=None, dz=None, dk=None):
        xx = x if dx is None else dx
        yy = y if dy is None else dy
        zz = z if dz is None else dz
        kk = k if dk is None else dk
        return (yy * NZ + zz, xx * 2 + kk)

    near_devices = [dev(dx=xp), dev(dx=xm), dev(dx=x2), dev(dk=1 - k)]
    near_devices += [dev(dz=up(n)) for n in (1, -1, 2, -2)]
    for yy in (yp, ym, y2):
        near_devices += [dev(dy=yy, dz=up(n)) for n in (0, 2, -2)]
    barrier = pltpu.get_barrier_semaphore()
    for d in near_devices:
        pl.semaphore_signal(barrier, inc=1, device_id=d, device_id_type=MESH)

    def send(src, dst, ss, rs_, target):
        pltpu.make_async_remote_copy(
            src_ref=src, dst_ref=dst, send_sem=ss, recv_sem=rs_, device_id=target, device_id_type=MESH
        ).start()

    def wait(ref, sem):
        pltpu.make_async_copy(ref, ref, sem).wait()

    def lanes(i):
        return pl.ds(pl.multiple_of(i * LANES, LANES), LANES)

    def shard(ox, core, oy):
        return (ox * 2 + core) * NY + oy

    def piece(r, owner):
        return r * NZ + owner

    cols = lanes(y)
    locals_ = [
        pltpu.make_async_copy(go, gobuf.at[shard(x, k, y)], loc_sem.at[0]),
        pltpu.make_async_copy(gate.at[:, cols], gtcv.at[y], loc_sem.at[1]),
        pltpu.make_async_copy(conv.at[:, cols], gtcv.at[NY + y], loc_sem.at[2]),
        pltpu.make_async_copy(rates.at[:, cols], rt, loc_sem.at[3]),
        pltpu.make_async_copy(residues.at[:, cols], rs, loc_sem.at[4]),
        pltpu.make_async_copy(weight.at[:, cols], wbuf.at[piece(0, z)], loc_sem.at[5]),
        pltpu.make_async_copy(rates, rt_all, loc_sem.at[6]),
        pltpu.make_async_copy(residues, rs_all, loc_sem.at[7]),
    ]
    for c in locals_:
        c.start()

    pl.semaphore_wait(barrier, len(near_devices))

    def z_slot(way, r, far):
        return r * NZ + (far if way else NZ - far)

    def z_send(way, r, owner, far, hop, src=None, to=None):
        ref = wbuf.at[piece(r, owner)]
        target = dev(dy=to, dz=up(-hop if way else hop))
        send(ref if src is None else src, ref, z_s.at[0], z_r.at[z_slot(way, r, far)], target)

    def z_wait(way, r, far):
        wait(wbuf.at[piece(r, up(far if way else -far))], z_r.at[z_slot(way, r, far)])

    for r in (0, 1, 3, 2):
        to = (y + NY - r) % NY
        src = weight.at[:, lanes(to)]
        for hop in (2, 1) if r == 0 else (2,):
            for way in (0, 1):
                z_send(way, r, z, hop, hop, src, to)
    for r in (1, 3, 2):
        to = (y + NY - r) % NY
        send(weight.at[:, lanes(to)], wbuf.at[piece(r, z)], z_s.at[0], z_r.at[r * NZ], dev(dy=to))

    A, B = (0, 64), (64, 64)
    A0, A1, B0, B1 = (0, 32), (32, 32), (64, 32), (96, 32)
    go_slots = {}

    def go_ref(ox, oy, part):
        return gobuf.at[shard(ox, k, oy), pl.ds(part[0], part[1]), :]

    def go_send(key, ox, oy, part, target, src=None):
        slot = go_slots.setdefault(key, len(go_slots))
        ref = go_ref(ox, oy, part)
        send(ref if src is None else src, ref, go_s.at[0], go_r.at[slot], target)

    def go_wait(key, ox, oy, part):
        wait(go_ref(ox, oy, part), go_r.at[go_slots[key]])

    one_way = (("L", dev(dx=xp)), ("R", dev(dx=xm)), ("X2", dev(dx=x2)))
    other_way = (("D", dev(dy=yp)), ("U", dev(dy=ym)), ("Y2", dev(dy=y2)))
    for near_part, far_part in ((A, B), (B, A)):
        for way, part in ((one_way, near_part), (other_way, far_part)):
            for key, target in way:
                go_send((key, part), x, y, part, target, go.at[pl.ds(part[0], part[1]), :])

    sib_slots = []

    def sibling(ox, oy, src=None):
        ref = gobuf.at[shard(ox, k, oy)]
        send(ref if src is None else src, ref, go_s.at[0], sib_r.at[0], dev(dk=1 - k))
        sib_slots.append((ox, oy))

    sibling(x, y, go)

    def z_round(far):
        for r in (0, 1, 3, 2):
            for way in (0, 1):
                owner = up(far if way else -far)
                z_wait(way, r, far)
                if far < 6 or way == r % 2:
                    z_send(way, r, owner, far + 2, 2)
                z_send(way, r, owner, far + 1, 1)

    for r in (1, 3, 2):
        wait(wbuf.at[piece(r, z)], z_r.at[r * NZ])
        for way in (0, 1):
            z_send(way, r, z, 1, 1)
    z_round(2)
    for r in range(1, NY):
        to = (y + r) % NY
        send(gate.at[:, lanes(to)], gtcv.at[y], gc_s.at[0], gc_r.at[0], dev(dy=to))
        send(conv.at[:, lanes(to)], gtcv.at[NY + y], gc_s.at[0], gc_r.at[0], dev(dy=to))
    columns = (("L", xm), ("R", xp), ("X2", x2))
    lines_ = (("D", ym), ("U", yp), ("Y2", y2))

    def turn(i):
        key, ox = columns[i]
        go_wait((key, A), ox, y, A)
        go_send((key, "D"), ox, y, A, dev(dy=yp))
        go_send((key, "U"), ox, y, A, dev(dy=ym))
        key, oy = lines_[i]
        go_wait((key, B), x, oy, B)
        go_send((key, "L"), x, oy, B, dev(dx=xp))
        go_send((key, "R"), x, oy, B, dev(dx=xm))

    def onward(i):
        key, ox = columns[i]
        go_wait((key, "D"), ox, ym, A)
        go_send((key, "Y2"), ox, ym, A0, dev(dy=yp))
        go_wait((key, "U"), ox, yp, A)
        go_send((key, "Y2"), ox, yp, A1, dev(dy=ym))
        key, oy = lines_[i]
        go_wait((key, "L"), xm, oy, B)
        go_send((key, "X2"), xm, oy, B0, dev(dx=xp))
        go_wait((key, "R"), xp, oy, B)
        go_send((key, "X2"), xp, oy, B1, dev(dx=xm))

    turn(0)
    turn(1)
    turn(2)
    for c in locals_:
        c.wait()
    for m in range(MODES):
        dec[m] = jnp.broadcast_to(jnp.exp(-rt[m : m + 1, :]), (8, LANES))
        resb[m] = jnp.broadcast_to(rs[m : m + 1, :], (8, LANES))
    z_round(4)
    for i in range(3):
        key, ox = columns[i]
        go_wait((key, B), ox, y, B)
        sibling(ox, y)
        key, oy = lines_[i]
        go_wait((key, A), x, oy, A)
        sibling(x, oy)
    onward(0)
    onward(1)
    for ox in (xm, xp):
        for oy in (ym, yp):
            sibling(ox, oy)

    def spread(ref, m):
        rows = [jnp.broadcast_to(ref[m : m + 1, q * LANES : (q + 1) * LANES], (2, LANES)) for q in range(NY)]
        return jnp.concatenate(rows, axis=0)

    for m in range(MODES):
        dec_all[m] = jnp.exp(-spread(rt_all, m))
        resb_all[m] = spread(rs_all, m)
    z_round(6)
    onward(2)
    wait(gtcv.at[pl.ds(0, 6)], gc_r.at[0])
    cvf[...] = gtcv[NY : 2 * NY].reshape(NY * ROWS, LANES).astype(F32)

    def end_step(t, sums):
        c = cvf[pl.ds(t, 8, stride=SEG), :]
        return tuple(dec[m] * (s + c) for m, s in enumerate(sums))

    zeros = tuple(jnp.zeros((8, LANES), F32) for _ in range(MODES))
    for m, s in enumerate(lax.fori_loop(0, SEG, end_step, zeros)):
        ends[m] = s
    for i in range(2):
        key, ox = columns[i]
        go_wait((key, "Y2"), ox, y2, A)
        sibling(ox, y2)
        key, oy = lines_[i]
        go_wait((key, "X2"), x2, oy, B)
        sibling(x2, oy)
    go_wait(("X2", "Y2"), x2, y2, A)
    go_wait(("Y2", "X2"), x2, y2, B)
    sibling(x2, y2)
    for far in (1, 3, 5, 7, 8):
        for r in range(NY):
            for way in (0, 1):
                if far < 8 or way == r % 2:
                    z_wait(way, r, far)
    wait(gobuf.at[pl.ds(0, NX * NY)], sib_r.at[0])

    total = jnp.zeros((NY * ROWS, LANES), F32)
    for ox in range(NX):
        rel = (ox + NY - y) % NY
        for half in range(2):
            a = gobuf[(ox * 2 + half) * NY : (ox * 2 + half + 1) * NY].reshape(NY * ROWS, WIDE)
            w = wbuf[pl.ds(rel * NZ + half * 8, 8)].reshape(WIDE, LANES)
            total = total + jnp.dot(a, w, preferred_element_type=F32)
    gc[...] = total * gtcv[:NY].reshape(NY * ROWS, LANES).astype(F32)

    def start_step(i, sums):
        g = gc[pl.ds(SEG - 1 - i, 8, stride=SEG), :]
        return tuple(dec[m] * s + g for m, s in enumerate(sums))

    row = lax.broadcasted_iota(jnp.int32, (8, LANES), 0)
    even = row % 2 == 0

    def by_seg(m):
        return jnp.broadcast_to(jnp.exp(-rt[m : m + 1, :] * F32(SEG)), (8, LANES))

    def next_up(v):
        return pltpu.roll(v, 7, 0)

    def next_down(v):
        return pltpu.roll(v, 1, 0)

    half_modes = MODES // 2
    sums = lax.fori_loop(0, SEG, start_step, zeros)
    for p in range(half_modes):
        s, o = sums[p], sums[p + half_modes]
        sent[p] = jnp.where(even, s + by_seg(p) * next_up(s), next_down(o) + by_seg(p + half_modes) * o)

    far_first = [8]
    for d in range(7, 0, -1):
        far_first += [d, -d]

    arrived[z] = sent[z % half_modes]
    for d in far_first:
        send(sent.at[up(d) % half_modes], arrived.at[z], a_s.at[0], a_r.at[0], dev(dz=up(d)))
    for p in range(half_modes):
        s, o = ends[p], ends[p + half_modes]
        sent_end[p] = jnp.where(even, next_up(s) + by_seg(p) * s, o + by_seg(p + half_modes) * next_down(o))
    arrived_end[z] = sent_end[z % half_modes]
    for d in far_first:
        send(sent_end.at[up(d) % half_modes], arrived_end.at[z], e_s.at[0], e_r.at[0], dev(dz=up(d)))

    def near_step(i, carry):
        sums, inner = carry
        t = SEG - 1 - i
        g = gc[pl.ds(t, 8, stride=SEG), :]
        c = cvf[pl.ds(t, 8, stride=SEG), :]
        sums = tuple(dec[m] * s + g for m, s in enumerate(sums))
        inner = tuple(n + c * s for n, s in zip(inner, sums))
        acc = resb[0] * sums[0]
        for m in range(1, MODES):
            acc = acc + resb[m] * sums[m]
        nearf[pl.ds(t, 8, stride=SEG), :] = acc
        return sums, inner

    from_second = tuple(jnp.where(even, next_up(s), 0.0) for s in sums)
    _, inner = lax.fori_loop(0, SEG, near_step, (from_second, zeros))
    for m in range(MODES):
        inrow[m % half_modes, m // half_modes : m // half_modes + 1, :] = jnp.sum(inner[m], axis=0, keepdims=True)
    inrow_in[z] = inrow[z % half_modes]
    for d in far_first:
        send(inrow.at[up(d) % half_modes], inrow_in.at[z], i_s.at[0], i_r.at[0], dev(dz=up(d)))
    for r in (2, 1, 3):
        to = (y + r) % NY
        rows = pl.ds(pl.multiple_of(to * ROWS, ROWS), ROWS)
        mine = pl.ds(pl.multiple_of(y * ROWS, ROWS), ROWS)
        send(nearf.at[rows, :], near.at[mine, :], n_s.at[0], n_r.at[0], dev(dy=to))
    near[mine, :] = nearf[mine, :]

    pair = z % half_modes
    rate = jnp.where(even, rt[pl.ds(pair, 1), :], rt[pl.ds(pair + half_modes, 1), :])
    by_block = jnp.exp(-rate * F32(ROWS))
    by_line = jnp.exp(-rate * F32(ROWS * NZ))
    to_line = [jnp.exp(-rate * F32(ROWS * (NZ - 1 - zz))) for zz in range(NZ)]
    wait(arrived.at[pl.ds(0, NZ - 1)], a_r.at[0])
    after = [None] * NZ
    after[NZ - 1] = jnp.zeros((8, LANES), F32)
    for zz in range(NZ - 2, -1, -1):
        after[zz] = arrived[zz + 1] + by_block * after[zz + 1]
    line = arrived[0] + by_block * after[0]

    def next_line(v):
        return jnp.where(row < 6, pltpu.roll(v, 6, 0), 0.0)

    line_next = next_line(line)
    lines = line_next
    for _ in range(NY - 2):
        lines = line_next + by_line * next_line(lines)
    ins = []
    for zz in range(NZ):
        ins.append(after[zz] + to_line[zz] * lines)
        for b in range(NY):
            backs[zz * NY + b] = ins[zz][2 * b : 2 * b + 2]

    served = (-4, 3, -3, 2, -2, 1, -1, 0)
    slot = pair * NY + y
    incoming[slot] = backs[z * NY + y]
    for d in served:
        for r in (2, 1, 3, 0):
            if d or r:
                to = (y + r) % NY
                send(backs.at[up(d) * NY + to], incoming.at[slot], b_s.at[0], b_r.at[0], dev(dy=to, dz=up(d)))

    wait(arrived_end.at[pl.ds(0, NZ - 1)], e_r.at[0])
    grad = jnp.zeros((8, LANES), F32)
    for zz in range(NZ):
        grad = grad + arrived_end[zz] * ins[zz]
    grad = grad + pltpu.roll(grad, 4, 0)
    grad = (grad + pltpu.roll(grad, 2, 0))[:2]
    wait(inrow_in.at[pl.ds(0, NZ - 1)], i_r.at[0])
    for zz in range(NZ):
        grad = grad + inrow_in[zz]
    rowsum[...] = grad * F32(1.0 / LENGTH)
    rowsum_in[slot] = rowsum[...]
    for d in served:
        for r in (2, 1, 3, 0):
            if d or r:
                to = (y + r) % NY
                send(rowsum, rowsum_in.at[slot], t_s.at[0], t_r.at[0], dev(dy=to, dz=up(d)))

    wait(near.at[pl.ds(0, 3 * ROWS), :], n_r.at[0])
    wait(incoming.at[pl.ds(0, half_modes * NY - 1)], b_r.at[0])
    carried = [None] * MODES
    for p in range(half_modes):
        both = jnp.concatenate([incoming[p * NY + q] for q in range(NY)], axis=0)
        for m, late in (
            (p, jnp.where(even, both, next_down(both))),
            (p + half_modes, jnp.where(even, next_up(both), both)),
        ):
            carried[m] = jnp.where(even, jnp.exp(-spread(rt_all, m) * F32(SEG)) * late, late)

    def far_step(i, sums):
        t = SEG - 1 - i
        sums = tuple(dec_all[m] * s for m, s in enumerate(sums))
        acc = near[pl.ds(t, 8, stride=SEG), :]
        for m in range(MODES):
            acc = acc + resb_all[m] * sums[m]
        outf[pl.ds(t, 8, stride=SEG), :] = acc
        return sums

    lax.fori_loop(0, SEG, far_step, tuple(carried))
    for q in range(NY):
        out[:, q * LANES : (q + 1) * LANES] = outf[q * ROWS : (q + 1) * ROWS, :].astype(BF16)

    wait(rowsum_in.at[pl.ds(0, half_modes * NY - 1)], t_r.at[0])
    for m in range(MODES):
        for q in range(NY):
            j = m // half_modes
            rout[m : m + 1, q * LANES : (q + 1) * LANES] = rowsum_in[(m % half_modes) * NY + q, j : j + 1, :]

    wait(gobuf.at[pl.ds(0, 31)], go_s.at[0])
    wait(wbuf.at[pl.ds(0, 63)], z_s.at[0])
    wait(gtcv.at[pl.ds(0, 6)], gc_s.at[0])
    wait(arrived.at[pl.ds(0, NZ - 1)], a_s.at[0])
    wait(arrived.at[pl.ds(0, NZ - 1)], e_s.at[0])
    wait(inrow_in.at[pl.ds(0, NZ - 1)], i_s.at[0])
    wait(near.at[pl.ds(0, 3 * ROWS), :], n_s.at[0])
    wait(incoming.at[pl.ds(0, 31)], b_s.at[0])
    wait(incoming.at[pl.ds(0, 31)], t_s.at[0])


def local(grad_out, gate, conv_input, out_weight, residues, rates):
    hbm = pl.BlockSpec(memory_space=pltpu.HBM)
    vmem = pl.BlockSpec(memory_space=pltpu.VMEM)
    dma = pltpu.SemaphoreType.DMA

    def f32(*shape):
        return pltpu.VMEM(shape, F32)

    def bf16(*shape):
        return pltpu.VMEM(shape, BF16)

    return pl.pallas_call(
        kernel,
        name="modal_backward",
        out_shape=(
            jax.ShapeDtypeStruct((ROWS, WIDE), BF16),
            jax.ShapeDtypeStruct((MODES, WIDE), F32),
        ),
        in_specs=[hbm] * 6,
        out_specs=(vmem, vmem),
        scratch_shapes=[
            bf16(2 * NX * NY, ROWS, WIDE),
            bf16(NY * NZ, 64, LANES),
            bf16(2 * NY, ROWS, LANES),
            f32(MODES, LANES),
            f32(MODES, LANES),
            f32(MODES, WIDE),
            f32(MODES, WIDE),
            f32(MODES, 8, LANES),
            f32(MODES, 8, LANES),
            f32(MODES, 8, LANES),
            f32(MODES, 8, LANES),
            f32(NY * ROWS, LANES),
            f32(NY * ROWS, LANES),
            f32(NY * ROWS, LANES),
            f32(NY * ROWS, LANES),
            f32(MODES, 8, LANES),
            f32(MODES, 8, LANES),
            f32(MODES // 2, 8, LANES),
            f32(NZ, 8, LANES),
            f32(MODES // 2, 8, LANES),
            f32(NZ, 8, LANES),
            f32(MODES // 2, 2, LANES),
            f32(NZ, 2, LANES),
            f32(NZ * NY, 2, LANES),
            f32(MODES // 2 * NY, 2, LANES),
            f32(2, LANES),
            f32(MODES // 2 * NY, 2, LANES),
            f32(NY * ROWS, LANES),
            dma((8,)),
            dma((1,)), dma((30,)), dma((1,)),
            dma((1,)), dma((NY * NZ,)),
            dma((1,)), dma((1,)),
            dma((1,)), dma((1,)),
            dma((1,)), dma((1,)),
            dma((1,)), dma((1,)),
            dma((1,)), dma((1,)),
            dma((1,)), dma((1,)),
            dma((1,)), dma((1,)),
        ],
        compiler_params=pltpu.CompilerParams(
            collective_id=1, has_side_effects=True, vmem_limit_bytes=63 << 20
        ),
    )(grad_out, gate, conv_input, out_weight.T, residues, rates)


def solution(mesh):
    placed = (
        P("ctx", "tp"),
        P("ctx", "tp"),
        P("ctx", "tp"),
        P("tp", "ctx"),
        P(None, "tp"),
        P(None, "tp"),
    )
    return jax.shard_map(
        local,
        mesh=mesh,
        in_specs=placed,
        out_specs=(P("ctx", "tp"), P(None, "tp")),
        check_vma=False,
    )
```

```python
import jax
import jax.numpy as jnp
from jax import lax
from jax.experimental import pallas as pl
from jax.experimental.pallas import tpu as pltpu
from jax.sharding import PartitionSpec as P

MESH = pl.DeviceIdType.MESH
F32 = jnp.float32
BF16 = jnp.bfloat16
MODES = 16
NX = 4
NY = 4
NZ = 16
ROWS = 128
WIDE = 512
LANES = 128
SEG = 64
LENGTH = 8192
HOPS = {0: (2, 1), 2: (2, 1), 4: (2, 1), 6: (2, 1)}


def kernel(
    go, gate, conv, weight, residues, rates,
    out, rout,
    gobuf, wbuf, gtcv, rt, rs, rt_all, rs_all,
    dec, resb, dec_all, resb_all, seg_all, gc, cvf, nearf, near, sent, arrived, sent_end, arrived_end,
    inrow, inrow_in, backs, incoming, rowsum, rowsum_in, outf,
    loc_sem, go_s, go_r, sib_r, z_s, z_r, gc_s, gc_r,
    a_s, a_r, e_s, e_r, i_s, i_r, n_s, n_r, b_s, b_r, t_s, t_r,
):
    ctx = lax.axis_index("ctx")
    tp = lax.axis_index("tp")
    x, k = tp // 2, tp % 2
    y, z = ctx // NZ, ctx % NZ
    xp, xm, x2 = (x + 1) % NX, (x + 3) % NX, (x + 2) % NX
    yp, ym, y2 = (y + 1) % NY, (y + 3) % NY, (y + 2) % NY

    def up(n):
        return (z + NZ + n) % NZ

    def dev(dx=None, dy=None, dz=None, dk=None):
        xx = x if dx is None else dx
        yy = y if dy is None else dy
        zz = z if dz is None else dz
        kk = k if dk is None else dk
        return (yy * NZ + zz, xx * 2 + kk)

    near_devices = [dev(dx=xp), dev(dx=xm), dev(dx=x2), dev(dk=1 - k)]
    near_devices += [dev(dz=up(n)) for n in (1, -1, 2, -2)]
    for yy in (yp, ym, y2):
        near_devices += [dev(dy=yy, dz=up(n)) for n in (0, 2, -2)]
    barrier = pltpu.get_barrier_semaphore()
    for d in near_devices:
        pl.semaphore_signal(barrier, inc=1, device_id=d, device_id_type=MESH)

    def send(src, dst, ss, rs_, target):
        pltpu.make_async_remote_copy(
            src_ref=src, dst_ref=dst, send_sem=ss, recv_sem=rs_, device_id=target, device_id_type=MESH
        ).start()

    def wait(ref, sem):
        pltpu.make_async_copy(ref, ref, sem).wait()

    def lanes(i):
        return pl.ds(pl.multiple_of(i * LANES, LANES), LANES)

    def shard(ox, core, oy):
        return (ox * 2 + core) * NY + oy

    def piece(r, owner):
        return r * NZ + owner

    cols = lanes(y)
    locals_ = [
        pltpu.make_async_copy(go, gobuf.at[shard(x, k, y)], loc_sem.at[0]),
        pltpu.make_async_copy(gate.at[:, cols], gtcv.at[y], loc_sem.at[1]),
        pltpu.make_async_copy(conv.at[:, cols], gtcv.at[NY + y], loc_sem.at[2]),
        pltpu.make_async_copy(rates.at[:, cols], rt, loc_sem.at[3]),
        pltpu.make_async_copy(residues.at[:, cols], rs, loc_sem.at[4]),
        pltpu.make_async_copy(weight.at[:, cols], wbuf.at[piece(0, z)], loc_sem.at[5]),
        pltpu.make_async_copy(rates, rt_all, loc_sem.at[6]),
        pltpu.make_async_copy(residues, rs_all, loc_sem.at[7]),
    ]
    for c in locals_:
        c.start()

    pl.semaphore_wait(barrier, len(near_devices))

    def z_slot(way, r, far):
        return r * NZ + (far if way else NZ - far)

    def z_send(way, r, owner, far, hop, src=None, to=None):
        ref = wbuf.at[piece(r, owner)]
        target = dev(dy=to, dz=up(-hop if way else hop))
        send(ref if src is None else src, ref, z_s.at[0], z_r.at[z_slot(way, r, far)], target)

    def z_wait(way, r, far):
        wait(wbuf.at[piece(r, up(far if way else -far))], z_r.at[z_slot(way, r, far)])

    for r in (0, 1, 3, 2):
        to = (y + NY - r) % NY
        src = weight.at[:, lanes(to)]
        for hop in HOPS[0] if r == 0 else HOPS[0][:1]:
            for way in (0, 1):
                z_send(way, r, z, hop, hop, src, to)
    for r in (1, 3, 2):
        to = (y + NY - r) % NY
        send(weight.at[:, lanes(to)], wbuf.at[piece(r, z)], z_s.at[0], z_r.at[r * NZ], dev(dy=to))

    A, B = (0, 48), (48, 80)
    A0, A1, B0, B1 = (0, 32), (32, 16), (48, 48), (96, 32)
    go_slots = {}

    def go_ref(ox, oy, part):
        return gobuf.at[shard(ox, k, oy), pl.ds(part[0], part[1]), :]

    def go_send(key, ox, oy, part, target, src=None):
        slot = go_slots.setdefault(key, len(go_slots))
        ref = go_ref(ox, oy, part)
        send(ref if src is None else src, ref, go_s.at[0], go_r.at[slot], target)

    def go_wait(key, ox, oy, part):
        wait(go_ref(ox, oy, part), go_r.at[go_slots[key]])

    one_way = (("L", dev(dx=xp)), ("R", dev(dx=xm)), ("X2", dev(dx=x2)))
    other_way = (("D", dev(dy=yp)), ("U", dev(dy=ym)), ("Y2", dev(dy=y2)))
    for near_part, far_part in ((A, B), (B, A)):
        for way, part in ((one_way, near_part), (other_way, far_part)):
            for key, target in way:
                go_send((key, part), x, y, part, target, go.at[pl.ds(part[0], part[1]), :])

    sib_slots = []

    def sibling(ox, oy, src=None):
        ref = gobuf.at[shard(ox, k, oy)]
        send(ref if src is None else src, ref, go_s.at[0], sib_r.at[0], dev(dk=1 - k))
        sib_slots.append((ox, oy))

    sibling(x, y, go)

    def z_round(far, pieces=(0, 1, 3, 2)):
        for r in pieces:
            for way in (0, 1):
                owner = up(far if way else -far)
                z_wait(way, r, far)
                for hop in HOPS[far]:
                    if far + hop < 8 or way == r % 2:
                        z_send(way, r, owner, far + hop, hop)

    def y_pieces():
        for r in (1, 3, 2):
            wait(wbuf.at[piece(r, z)], z_r.at[r * NZ])
            for way in (0, 1):
                z_send(way, r, z, 1, 1)

    columns = (("L", xm), ("R", xp), ("X2", x2))
    lines_ = (("D", ym), ("U", yp), ("Y2", y2))

    def turn(i):
        key, ox = columns[i]
        go_wait((key, A), ox, y, A)
        go_send((key, "D"), ox, y, A, dev(dy=yp))
        go_send((key, "U"), ox, y, A, dev(dy=ym))
        key, oy = lines_[i]
        go_wait((key, B), x, oy, B)
        go_send((key, "L"), x, oy, B, dev(dx=xp))
        go_send((key, "R"), x, oy, B, dev(dx=xm))

    def onward(i):
        key, ox = columns[i]
        go_wait((key, "D"), ox, ym, A)
        go_send((key, "Y2"), ox, ym, A0, dev(dy=yp))
        go_wait((key, "U"), ox, yp, A)
        go_send((key, "Y2"), ox, yp, A1, dev(dy=ym))
        key, oy = lines_[i]
        go_wait((key, "L"), xm, oy, B)
        go_send((key, "X2"), xm, oy, B0, dev(dx=xp))
        go_wait((key, "R"), xp, oy, B)
        go_send((key, "X2"), xp, oy, B1, dev(dx=xm))

    def gates():
        for r in range(1, NY):
            to = (y + r) % NY
            send(gate.at[:, lanes(to)], gtcv.at[y], gc_s.at[0], gc_r.at[0], dev(dy=to))
            send(conv.at[:, lanes(to)], gtcv.at[NY + y], gc_s.at[0], gc_r.at[0], dev(dy=to))

    def near_shards(i):
        key, ox = columns[i]
        go_wait((key, B), ox, y, B)
        sibling(ox, y)
        key, oy = lines_[i]
        go_wait((key, A), x, oy, A)
        sibling(x, oy)

    def diagonal_shards():
        for ox in (xm, xp):
            for oy in (ym, yp):
                sibling(ox, oy)

    def far_shards(i):
        key, ox = columns[i]
        go_wait((key, "Y2"), ox, y2, A)
        if i < 2:
            sibling(ox, y2)
        key, oy = lines_[i]
        go_wait((key, "X2"), x2, oy, B)
        sibling(x2, oy)

    def spread(ref, m):
        rows = [jnp.broadcast_to(ref[m : m + 1, q * LANES : (q + 1) * LANES], (2, LANES)) for q in range(NY)]
        return jnp.concatenate(rows, axis=0)

    def decays():
        for c in locals_:
            c.wait()
        for m in range(MODES):
            dec[m] = jnp.broadcast_to(jnp.exp(-rt[m : m + 1, :]), (8, LANES))
            resb[m] = jnp.broadcast_to(rs[m : m + 1, :], (8, LANES))
            rate = spread(rt_all, m)
            dec_all[m] = jnp.exp(-rate)
            seg_all[m] = jnp.exp(-rate * F32(SEG))
            resb_all[m] = spread(rs_all, m)

    row = lax.broadcasted_iota(jnp.int32, (8, LANES), 0)
    even = row % 2 == 0

    def by_seg(m):
        return jnp.broadcast_to(jnp.exp(-rt[m : m + 1, :] * F32(SEG)), (8, LANES))

    def next_up(v):
        return pltpu.roll(v, 7, 0)

    def next_down(v):
        return pltpu.roll(v, 1, 0)

    half_modes = MODES // 2
    far_first = [8]
    for d in range(7, 0, -1):
        far_first += [d, -d]

    zeros = tuple(jnp.zeros((8, LANES), F32) for _ in range(MODES))

    def end_step(t, sums):
        c = cvf[pl.ds(t, 8, stride=SEG), :]
        return tuple(dec[m] * (s + c) for m, s in enumerate(sums))

    def input_ends():
        wait(gtcv.at[pl.ds(0, 6)], gc_r.at[0])
        cvf[...] = gtcv[NY : 2 * NY].reshape(NY * ROWS, LANES).astype(F32)
        sums = lax.fori_loop(0, SEG, end_step, zeros)
        for p in range(half_modes):
            s, o = sums[p], sums[p + half_modes]
            sent_end[p] = jnp.where(even, next_up(s) + by_seg(p) * s, o + by_seg(p + half_modes) * next_down(o))
        arrived_end[z] = sent_end[z % half_modes]

    def send_ends(chips):
        for d in chips:
            send(sent_end.at[up(d) % half_modes], arrived_end.at[z], e_s.at[0], e_r.at[0], dev(dz=up(d)))

    def z_leaves(fars):
        for far in fars:
            for r in range(NY):
                for way in (0, 1):
                    if far < 8 or way == r % 2:
                        z_wait(way, r, far)

    z_round(2, (0,))
    turn(0)
    turn(1)
    z_round(2, (1, 3, 2))
    y_pieces()
    turn(2)
    gates()
    decays()
    near_shards(0)
    near_shards(1)
    near_shards(2)
    z_round(4, (0, 1))
    onward(0)
    z_round(4, (3, 2))
    onward(1)
    diagonal_shards()
    onward(2)
    input_ends()
    z_round(6, (0, 1))
    far_shards(0)
    z_round(6, (3, 2))
    z_leaves((1, 3, 5))
    send_ends((6, -6, 5, -5, 4, -4, 3, -3, 2, -2, 1, -1))
    far_shards(1)
    far_shards(2)
    z_leaves((7, 8))
    send_ends((8, 7, -7))
    wait(gobuf.at[pl.ds(0, NX * NY)], sib_r.at[0])

    total = jnp.zeros((NY * ROWS, LANES), F32)
    for ox in range(NX):
        rel = (ox + NY - y) % NY
        for half in range(2):
            a = gobuf[(ox * 2 + half) * NY : (ox * 2 + half + 1) * NY].reshape(NY * ROWS, WIDE)
            w = wbuf[pl.ds(rel * NZ + half * 8, 8)].reshape(WIDE, LANES)
            total = total + jnp.dot(a, w, preferred_element_type=F32)
    gc[...] = total * gtcv[:NY].reshape(NY * ROWS, LANES).astype(F32)

    def start_step(i, sums):
        g = gc[pl.ds(SEG - 1 - i, 8, stride=SEG), :]
        return tuple(dec[m] * s + g for m, s in enumerate(sums))

    sums = lax.fori_loop(0, SEG, start_step, zeros)
    for p in range(half_modes):
        s, o = sums[p], sums[p + half_modes]
        sent[p] = jnp.where(even, s + by_seg(p) * next_up(s), next_down(o) + by_seg(p + half_modes) * o)

    arrived[z] = sent[z % half_modes]
    for d in far_first:
        send(sent.at[up(d) % half_modes], arrived.at[z], a_s.at[0], a_r.at[0], dev(dz=up(d)))
    def inner_step(i, carry):
        sums, inner = carry
        g = gc[pl.ds(SEG - 1 - i, 8, stride=SEG), :]
        c = cvf[pl.ds(SEG - 1 - i, 8, stride=SEG), :]
        sums = tuple(dec[m] * s + g for m, s in enumerate(sums))
        return sums, tuple(n + c * s for n, s in zip(inner, sums))

    from_second = tuple(jnp.where(even, next_up(s), 0.0) for s in sums)
    _, inner = lax.fori_loop(0, SEG, inner_step, (from_second, zeros))
    for m in range(MODES):
        inrow[m % half_modes, m // half_modes : m // half_modes + 1, :] = jnp.sum(inner[m], axis=0, keepdims=True)
    inrow_in[z] = inrow[z % half_modes]
    for d in far_first:
        send(inrow.at[up(d) % half_modes], inrow_in.at[z], i_s.at[0], i_r.at[0], dev(dz=up(d)))

    def near_step(i, sums):
        t = SEG - 1 - i
        g = gc[pl.ds(t, 8, stride=SEG), :]
        sums = tuple(dec[m] * s + g for m, s in enumerate(sums))
        acc = resb[0] * sums[0]
        for m in range(1, MODES):
            acc = acc + resb[m] * sums[m]
        nearf[pl.ds(t, 8, stride=SEG), :] = acc
        return sums

    lax.fori_loop(0, SEG, near_step, from_second)
    for r in (2, 1, 3):
        to = (y + r) % NY
        rows = pl.ds(pl.multiple_of(to * ROWS, ROWS), ROWS)
        mine = pl.ds(pl.multiple_of(y * ROWS, ROWS), ROWS)
        send(nearf.at[rows, :], near.at[mine, :], n_s.at[0], n_r.at[0], dev(dy=to))
    near[mine, :] = nearf[mine, :]

    pair = z % half_modes
    rate = jnp.where(even, rt[pl.ds(pair, 1), :], rt[pl.ds(pair + half_modes, 1), :])
    by_block = jnp.exp(-rate * F32(ROWS))
    by_line = jnp.exp(-rate * F32(ROWS * NZ))
    to_line = [jnp.exp(-rate * F32(ROWS * (NZ - 1 - zz))) for zz in range(NZ)]
    wait(arrived.at[pl.ds(0, NZ - 1)], a_r.at[0])
    after = [None] * NZ
    after[NZ - 1] = jnp.zeros((8, LANES), F32)
    for zz in range(NZ - 2, -1, -1):
        after[zz] = arrived[zz + 1] + by_block * after[zz + 1]
    line = arrived[0] + by_block * after[0]

    def next_line(v):
        return jnp.where(row < 6, pltpu.roll(v, 6, 0), 0.0)

    line_next = next_line(line)
    lines = line_next
    for _ in range(NY - 2):
        lines = line_next + by_line * next_line(lines)
    ins = []
    for zz in range(NZ):
        ins.append(after[zz] + to_line[zz] * lines)
        for b in range(NY):
            backs[zz * NY + b] = ins[zz][2 * b : 2 * b + 2]

    served = (-4, 3, -3, 2, -2, 1, -1, 0)
    slot = pair * NY + y
    incoming[slot] = backs[z * NY + y]
    for d in served:
        for r in (2, 1, 3, 0):
            if d or r:
                to = (y + r) % NY
                send(backs.at[up(d) * NY + to], incoming.at[slot], b_s.at[0], b_r.at[0], dev(dy=to, dz=up(d)))

    wait(arrived_end.at[pl.ds(0, NZ - 1)], e_r.at[0])
    grad = jnp.zeros((8, LANES), F32)
    for zz in range(NZ):
        grad = grad + arrived_end[zz] * ins[zz]
    grad = grad + pltpu.roll(grad, 4, 0)
    grad = (grad + pltpu.roll(grad, 2, 0))[:2]
    wait(inrow_in.at[pl.ds(0, NZ - 1)], i_r.at[0])
    for zz in range(NZ):
        grad = grad + inrow_in[zz]
    rowsum[...] = grad * F32(1.0 / LENGTH)
    rowsum_in[slot] = rowsum[...]
    for d in served:
        for r in (2, 1, 3, 0):
            if d or r:
                to = (y + r) % NY
                send(rowsum, rowsum_in.at[slot], t_s.at[0], t_r.at[0], dev(dy=to, dz=up(d)))

    wait(near.at[pl.ds(0, 3 * ROWS), :], n_r.at[0])
    wait(incoming.at[pl.ds(0, half_modes * NY - 1)], b_r.at[0])
    carried = [None] * MODES
    for p in range(half_modes):
        both = jnp.concatenate([incoming[p * NY + q] for q in range(NY)], axis=0)
        for m, late in (
            (p, jnp.where(even, both, next_down(both))),
            (p + half_modes, jnp.where(even, next_up(both), both)),
        ):
            carried[m] = jnp.where(even, seg_all[m] * late, late)

    def far_step(i, sums):
        t = SEG - 1 - i
        sums = tuple(dec_all[m] * s for m, s in enumerate(sums))
        acc = near[pl.ds(t, 8, stride=SEG), :]
        for m in range(MODES):
            acc = acc + resb_all[m] * sums[m]
        outf[pl.ds(t, 8, stride=SEG), :] = acc
        return sums

    lax.fori_loop(0, SEG, far_step, tuple(carried))
    for q in range(NY):
        out[:, q * LANES : (q + 1) * LANES] = outf[q * ROWS : (q + 1) * ROWS, :].astype(BF16)

    wait(rowsum_in.at[pl.ds(0, half_modes * NY - 1)], t_r.at[0])
    for m in range(MODES):
        for q in range(NY):
            j = m // half_modes
            rout[m : m + 1, q * LANES : (q + 1) * LANES] = rowsum_in[(m % half_modes) * NY + q, j : j + 1, :]

    wait(gobuf.at[pl.ds(0, 31)], go_s.at[0])
    wait(wbuf.at[pl.ds(0, 63)], z_s.at[0])
    wait(gtcv.at[pl.ds(0, 6)], gc_s.at[0])
    wait(arrived.at[pl.ds(0, NZ - 1)], a_s.at[0])
    wait(arrived.at[pl.ds(0, NZ - 1)], e_s.at[0])
    wait(inrow_in.at[pl.ds(0, NZ - 1)], i_s.at[0])
    wait(near.at[pl.ds(0, 3 * ROWS), :], n_s.at[0])
    wait(incoming.at[pl.ds(0, 31)], b_s.at[0])
    wait(incoming.at[pl.ds(0, 31)], t_s.at[0])


def local(grad_out, gate, conv_input, out_weight, residues, rates):
    hbm = pl.BlockSpec(memory_space=pltpu.HBM)
    vmem = pl.BlockSpec(memory_space=pltpu.VMEM)
    dma = pltpu.SemaphoreType.DMA

    def f32(*shape):
        return pltpu.VMEM(shape, F32)

    def bf16(*shape):
        return pltpu.VMEM(shape, BF16)

    operands = (grad_out, gate, conv_input, out_weight.T, residues, rates)
    operands = [pltpu.with_memory_space_constraint(a, pltpu.HBM) for a in operands]
    return pl.pallas_call(
        kernel,
        name="modal_backward",
        out_shape=(
            jax.ShapeDtypeStruct((ROWS, WIDE), BF16),
            jax.ShapeDtypeStruct((MODES, WIDE), F32),
        ),
        in_specs=[hbm] * 6,
        out_specs=(vmem, vmem),
        scratch_shapes=[
            bf16(2 * NX * NY, ROWS, WIDE),
            bf16(NY * NZ, 64, LANES),
            bf16(2 * NY, ROWS, LANES),
            f32(MODES, LANES),
            f32(MODES, LANES),
            f32(MODES, WIDE),
            f32(MODES, WIDE),
            f32(MODES, 8, LANES),
            f32(MODES, 8, LANES),
            f32(MODES, 8, LANES),
            f32(MODES, 8, LANES),
            f32(MODES, 8, LANES),
            f32(NY * ROWS, LANES),
            f32(NY * ROWS, LANES),
            f32(NY * ROWS, LANES),
            f32(NY * ROWS, LANES),
            f32(MODES // 2, 8, LANES),
            f32(NZ, 8, LANES),
            f32(MODES // 2, 8, LANES),
            f32(NZ, 8, LANES),
            f32(MODES // 2, 2, LANES),
            f32(NZ, 2, LANES),
            f32(NZ * NY, 2, LANES),
            f32(MODES // 2 * NY, 2, LANES),
            f32(2, LANES),
            f32(MODES // 2 * NY, 2, LANES),
            f32(NY * ROWS, LANES),
            dma((8,)),
            dma((1,)), dma((30,)), dma((1,)),
            dma((1,)), dma((NY * NZ,)),
            dma((1,)), dma((1,)),
            dma((1,)), dma((1,)),
            dma((1,)), dma((1,)),
            dma((1,)), dma((1,)),
            dma((1,)), dma((1,)),
            dma((1,)), dma((1,)),
            dma((1,)), dma((1,)),
        ],
        compiler_params=pltpu.CompilerParams(
            collective_id=1, has_side_effects=True, vmem_limit_bytes=32 << 20
        ),
    )(*operands)


def solution(mesh):
    placed = (
        P("ctx", "tp"),
        P("ctx", "tp"),
        P("ctx", "tp"),
        P("tp", "ctx"),
        P(None, "tp"),
        P(None, "tp"),
    )
    return jax.shard_map(
        local,
        mesh=mesh,
        in_specs=placed,
        out_specs=(P("ctx", "tp"), P(None, "tp")),
        check_vma=False,
    )
```

```python
import jax
import jax.numpy as jnp
from jax import lax
from jax.experimental import pallas as pl
from jax.experimental.pallas import tpu as pltpu
from jax.sharding import PartitionSpec as P

MESH = pl.DeviceIdType.MESH
F32 = jnp.float32
BF16 = jnp.bfloat16
MODES = 16
NX = 4
NY = 4
NZ = 16
ROWS = 128
WIDE = 512
LANES = 128
SEG = 64
LENGTH = 8192
UNROLL = 4
HOPS = {0: (2, 1), 2: (2, 1), 4: (2, 1), 6: (2, 1)}


def kernel(
    go, gate, conv, weight, residues, rates,
    out, rout,
    gobuf, wbuf, gtcv, rt, rs, rt_all, rs_all,
    dec, resb, dec_all, resb_all, seg_all, gc, cvf, nearf, near, heads, ends, sent, arrived, sent_end, arrived_end,
    inrow, inrow_in, backs, incoming, rowsum, rowsum_in, outf,
    loc_sem, go_s, go_r, sib_r, z_s, z_r, leaf_r, y_r, gc_s, gc_r,
    a_s, a_r, e_s, e_r, i_s, i_r, n_s, n_r, b_s, b_r, t_s, t_r,
):
    ctx = lax.axis_index("ctx")
    tp = lax.axis_index("tp")
    x, k = tp // 2, tp % 2
    y, z = ctx // NZ, ctx % NZ
    xp, xm, x2 = (x + 1) % NX, (x + 3) % NX, (x + 2) % NX
    yp, ym, y2 = (y + 1) % NY, (y + 3) % NY, (y + 2) % NY

    def up(n):
        return (z + NZ + n) % NZ

    def dev(dx=None, dy=None, dz=None, dk=None):
        xx = x if dx is None else dx
        yy = y if dy is None else dy
        zz = z if dz is None else dz
        kk = k if dk is None else dk
        return (yy * NZ + zz, xx * 2 + kk)

    near_devices = [dev(dx=xp), dev(dx=xm), dev(dx=x2), dev(dk=1 - k)]
    near_devices += [dev(dz=up(n)) for n in (1, -1, 2, -2)]
    for yy in (yp, ym, y2):
        near_devices += [dev(dy=yy, dz=up(n)) for n in (0, 2, -2)]
    barrier = pltpu.get_barrier_semaphore()
    for d in near_devices:
        pl.semaphore_signal(barrier, inc=1, device_id=d, device_id_type=MESH)

    def send(src, dst, ss, rs_, target):
        pltpu.make_async_remote_copy(
            src_ref=src, dst_ref=dst, send_sem=ss, recv_sem=rs_, device_id=target, device_id_type=MESH
        ).start()

    def wait(ref, sem):
        pltpu.make_async_copy(ref, ref, sem).wait()

    def lanes(i):
        return pl.ds(pl.multiple_of(i * LANES, LANES), LANES)

    def shard(ox, core, oy):
        return (ox * 2 + core) * NY + oy

    def piece(r, owner):
        return r * NZ + owner

    cols = lanes(y)
    locals_ = [
        pltpu.make_async_copy(go, gobuf.at[shard(x, k, y)], loc_sem.at[0]),
        pltpu.make_async_copy(gate.at[:, cols], gtcv.at[y], loc_sem.at[1]),
        pltpu.make_async_copy(conv.at[:, cols], gtcv.at[NY + y], loc_sem.at[2]),
        pltpu.make_async_copy(rates.at[:, cols], rt, loc_sem.at[3]),
        pltpu.make_async_copy(residues.at[:, cols], rs, loc_sem.at[4]),
        pltpu.make_async_copy(weight.at[:, cols], wbuf.at[piece(0, z)], loc_sem.at[5]),
        pltpu.make_async_copy(rates, rt_all, loc_sem.at[6]),
        pltpu.make_async_copy(residues, rs_all, loc_sem.at[7]),
    ]
    for c in locals_:
        c.start()

    pl.semaphore_wait(barrier, len(near_devices))

    def z_slot(way, r, far):
        return (r * 2 + way) * 3 + far // 2 - 1

    def z_send(way, r, owner, far, hop, src=None, to=None):
        ref = wbuf.at[piece(r, owner)]
        target = dev(dy=to, dz=up(-hop if way else hop))
        if far in HOPS:
            sem = z_r.at[z_slot(way, r, far)]
        else:
            sem = leaf_r.at[0 if far < 6 else 1]
        send(ref if src is None else src, ref, z_s.at[0], sem, target)

    def z_wait(way, r, far):
        wait(wbuf.at[piece(r, up(far if way else -far))], z_r.at[z_slot(way, r, far)])

    for r in (0, 1, 3, 2):
        to = (y + NY - r) % NY
        src = weight.at[:, lanes(to)]
        for hop in HOPS[0] if r == 0 else HOPS[0][:1]:
            for way in (0, 1):
                z_send(way, r, z, hop, hop, src, to)
    for r in (1, 3, 2):
        to = (y + NY - r) % NY
        send(weight.at[:, lanes(to)], wbuf.at[piece(r, z)], z_s.at[0], y_r.at[r], dev(dy=to))

    A, B = (0, 48), (48, 80)
    A0, A1, B0, B1 = (0, 32), (32, 16), (48, 48), (96, 32)
    go_slots = {}

    def go_ref(ox, oy, part):
        return gobuf.at[shard(ox, k, oy), pl.ds(part[0], part[1]), :]

    def go_send(key, ox, oy, part, target, src=None):
        slot = go_slots.setdefault(key, len(go_slots))
        ref = go_ref(ox, oy, part)
        send(ref if src is None else src, ref, go_s.at[0], go_r.at[slot], target)

    def go_wait(key, ox, oy, part):
        wait(go_ref(ox, oy, part), go_r.at[go_slots[key]])

    one_way = (("L", dev(dx=xp)), ("R", dev(dx=xm)), ("X2", dev(dx=x2)))
    other_way = (("D", dev(dy=yp)), ("U", dev(dy=ym)), ("Y2", dev(dy=y2)))
    for near_part, far_part in ((A, B), (B, A)):
        for way, part in ((one_way, near_part), (other_way, far_part)):
            for key, target in way:
                go_send((key, part), x, y, part, target, go.at[pl.ds(part[0], part[1]), :])

    sib_slots = []

    def sibling(ox, oy, src=None):
        ref = gobuf.at[shard(ox, k, oy)]
        send(ref if src is None else src, ref, go_s.at[0], sib_r.at[0], dev(dk=1 - k))
        sib_slots.append((ox, oy))

    sibling(x, y, go)

    def z_round(far, pieces=(0, 1, 3, 2)):
        for r in pieces:
            for way in (0, 1):
                owner = up(far if way else -far)
                z_wait(way, r, far)
                for hop in HOPS[far]:
                    if far + hop < 8 or way == r % 2:
                        z_send(way, r, owner, far + hop, hop)

    def y_pieces():
        for r in (1, 3, 2):
            wait(wbuf.at[piece(r, z)], y_r.at[r])
            for way in (0, 1):
                z_send(way, r, z, 1, 1)

    columns = (("L", xm), ("R", xp), ("X2", x2))
    lines_ = (("D", ym), ("U", yp), ("Y2", y2))

    def turn(i):
        key, ox = columns[i]
        go_wait((key, A), ox, y, A)
        go_send((key, "D"), ox, y, A, dev(dy=yp))
        go_send((key, "U"), ox, y, A, dev(dy=ym))
        key, oy = lines_[i]
        go_wait((key, B), x, oy, B)
        go_send((key, "L"), x, oy, B, dev(dx=xp))
        go_send((key, "R"), x, oy, B, dev(dx=xm))

    def onward(i):
        key, ox = columns[i]
        go_wait((key, "D"), ox, ym, A)
        go_send((key, "Y2"), ox, ym, A0, dev(dy=yp))
        go_wait((key, "U"), ox, yp, A)
        go_send((key, "Y2"), ox, yp, A1, dev(dy=ym))
        key, oy = lines_[i]
        go_wait((key, "L"), xm, oy, B)
        go_send((key, "X2"), xm, oy, B0, dev(dx=xp))
        go_wait((key, "R"), xp, oy, B)
        go_send((key, "X2"), xp, oy, B1, dev(dx=xm))

    def gates():
        for r in range(1, NY):
            to = (y + r) % NY
            send(gate.at[:, lanes(to)], gtcv.at[y], gc_s.at[0], gc_r.at[0], dev(dy=to))
            send(conv.at[:, lanes(to)], gtcv.at[NY + y], gc_s.at[0], gc_r.at[0], dev(dy=to))

    def near_shards(i):
        key, ox = columns[i]
        go_wait((key, B), ox, y, B)
        sibling(ox, y)
        key, oy = lines_[i]
        go_wait((key, A), x, oy, A)
        sibling(x, oy)

    def diagonal_shards():
        for ox in (xm, xp):
            for oy in (ym, yp):
                sibling(ox, oy)

    def far_shards(i):
        key, ox = columns[i]
        go_wait((key, "Y2"), ox, y2, A)
        if i < 2:
            sibling(ox, y2)
        key, oy = lines_[i]
        go_wait((key, "X2"), x2, oy, B)
        sibling(x2, oy)

    def spread(ref, m):
        rows = [jnp.broadcast_to(ref[m : m + 1, q * LANES : (q + 1) * LANES], (2, LANES)) for q in range(NY)]
        return jnp.concatenate(rows, axis=0)

    def decays():
        for c in locals_:
            c.wait()
        for m in range(MODES):
            dec[m] = jnp.broadcast_to(jnp.exp(-rt[m : m + 1, :]), (8, LANES))
            resb[m] = jnp.broadcast_to(rs[m : m + 1, :], (8, LANES))
            rate = spread(rt_all, m)
            dec_all[m] = jnp.exp(-rate)
            seg_all[m] = jnp.exp(-rate * F32(SEG))
            resb_all[m] = spread(rs_all, m)

    row = lax.broadcasted_iota(jnp.int32, (8, LANES), 0)
    even = row % 2 == 0

    def by_seg(m):
        return jnp.broadcast_to(jnp.exp(-rt[m : m + 1, :] * F32(SEG)), (8, LANES))

    def next_up(v):
        return pltpu.roll(v, 7, 0)

    def next_down(v):
        return pltpu.roll(v, 1, 0)

    half_modes = MODES // 2
    far_first = [8]
    for d in range(7, 0, -1):
        far_first += [d, -d]

    zeros = tuple(jnp.zeros((8, LANES), F32) for _ in range(MODES))

    def head_step(t, sums):
        c = cvf[pl.ds(t, 8, stride=SEG), :]
        sums = tuple(dec[m] * s + c for m, s in enumerate(sums))
        for m, s in enumerate(sums):
            heads[t, m] = s
        return sums

    def input_ends():
        wait(gtcv.at[pl.ds(0, 6)], gc_r.at[0])
        cvf[...] = gtcv[NY : 2 * NY].reshape(NY * ROWS, LANES).astype(F32)
        sums = lax.fori_loop(0, SEG, head_step, zeros)
        sums = [dec[m] * s for m, s in enumerate(sums)]
        for m, s in enumerate(sums):
            ends[m] = s
        for p in range(half_modes):
            s, o = sums[p], sums[p + half_modes]
            sent_end[p] = jnp.where(even, next_up(s) + by_seg(p) * s, o + by_seg(p + half_modes) * next_down(o))
        arrived_end[z] = sent_end[z % half_modes]

    def send_ends(chips):
        for d in chips:
            send(sent_end.at[up(d) % half_modes], arrived_end.at[z], e_s.at[0], e_r.at[0], dev(dz=up(d)))

    def z_leaves(group):
        wait(wbuf.at[pl.ds(0, 24 if group == 0 else 12)], leaf_r.at[group])

    z_round(2, (0,))
    turn(0)
    turn(1)
    z_round(2, (1, 3, 2))
    y_pieces()
    turn(2)
    gates()
    decays()
    near_shards(0)
    near_shards(1)
    near_shards(2)
    z_round(4, (0, 1))
    onward(0)
    z_round(4, (3, 2))
    onward(1)
    diagonal_shards()
    onward(2)
    input_ends()
    z_round(6, (0, 1))
    far_shards(0)
    z_round(6, (3, 2))
    z_leaves(0)
    send_ends((6, -6, 5, -5, 4, -4, 3, -3, 2, -2, 1, -1))
    far_shards(1)
    far_shards(2)
    z_leaves(1)
    send_ends((8, 7, -7))
    wait(gobuf.at[pl.ds(0, NX * NY)], sib_r.at[0])

    total = jnp.zeros((NY * ROWS, LANES), F32)
    for ox in range(NX):
        rel = (ox + NY - y) % NY
        for half in range(2):
            a = gobuf[(ox * 2 + half) * NY : (ox * 2 + half + 1) * NY].reshape(NY * ROWS, WIDE)
            w = wbuf[pl.ds(rel * NZ + half * 8, 8)].reshape(WIDE, LANES)
            total = total + jnp.dot(a, w, preferred_element_type=F32)
    gc[...] = total * gtcv[:NY].reshape(NY * ROWS, LANES).astype(F32)

    def start_step(i, sums):
        g = gc[pl.ds(SEG - 1 - i, 8, stride=SEG), :]
        return tuple(dec[m] * s + g for m, s in enumerate(sums))

    sums = lax.fori_loop(0, SEG, start_step, zeros, unroll=UNROLL)
    for p in range(half_modes):
        s, o = sums[p], sums[p + half_modes]
        sent[p] = jnp.where(even, s + by_seg(p) * next_up(s), next_down(o) + by_seg(p + half_modes) * o)

    arrived[z] = sent[z % half_modes]
    for d in far_first:
        send(sent.at[up(d) % half_modes], arrived.at[z], a_s.at[0], a_r.at[0], dev(dz=up(d)))
    def inner_step(t, inner):
        g = gc[pl.ds(t, 8, stride=SEG), :]
        return tuple(n + g * heads[t, m] for m, n in enumerate(inner))

    inner = lax.fori_loop(0, SEG, inner_step, zeros, unroll=UNROLL)
    from_second = tuple(jnp.where(even, next_up(s), 0.0) for s in sums)
    inner = [n + ends[m] * s for m, (n, s) in enumerate(zip(inner, from_second))]
    for m in range(MODES):
        inrow[m % half_modes, m // half_modes : m // half_modes + 1, :] = jnp.sum(inner[m], axis=0, keepdims=True)
    inrow_in[z] = inrow[z % half_modes]
    for d in far_first:
        send(inrow.at[up(d) % half_modes], inrow_in.at[z], i_s.at[0], i_r.at[0], dev(dz=up(d)))

    def near_step(i, sums):
        t = SEG - 1 - i
        g = gc[pl.ds(t, 8, stride=SEG), :]
        sums = tuple(dec[m] * s + g for m, s in enumerate(sums))
        acc = resb[0] * sums[0]
        for m in range(1, MODES):
            acc = acc + resb[m] * sums[m]
        nearf[pl.ds(t, 8, stride=SEG), :] = acc
        return sums

    lax.fori_loop(0, SEG, near_step, from_second, unroll=UNROLL)
    for r in (2, 1, 3):
        to = (y + r) % NY
        rows = pl.ds(pl.multiple_of(to * ROWS, ROWS), ROWS)
        mine = pl.ds(pl.multiple_of(y * ROWS, ROWS), ROWS)
        send(nearf.at[rows, :], near.at[mine, :], n_s.at[0], n_r.at[0], dev(dy=to))
    near[mine, :] = nearf[mine, :]

    pair = z % half_modes
    rate = jnp.where(even, rt[pl.ds(pair, 1), :], rt[pl.ds(pair + half_modes, 1), :])
    by_block = jnp.exp(-rate * F32(ROWS))
    by_line = jnp.exp(-rate * F32(ROWS * NZ))
    to_line = [jnp.exp(-rate * F32(ROWS * (NZ - 1 - zz))) for zz in range(NZ)]
    wait(arrived.at[pl.ds(0, NZ - 1)], a_r.at[0])
    after = [None] * NZ
    after[NZ - 1] = jnp.zeros((8, LANES), F32)
    for zz in range(NZ - 2, -1, -1):
        after[zz] = arrived[zz + 1] + by_block * after[zz + 1]
    line = arrived[0] + by_block * after[0]

    def next_line(v):
        return jnp.where(row < 6, pltpu.roll(v, 6, 0), 0.0)

    line_next = next_line(line)
    lines = line_next
    for _ in range(NY - 2):
        lines = line_next + by_line * next_line(lines)
    ins = []
    for zz in range(NZ):
        ins.append(after[zz] + to_line[zz] * lines)
        for b in range(NY):
            backs[zz * NY + b] = ins[zz][2 * b : 2 * b + 2]

    served = (-4, 3, -3, 2, -2, 1, -1, 0)
    slot = pair * NY + y
    incoming[slot] = backs[z * NY + y]
    for d in served:
        for r in (2, 1, 3, 0):
            if d or r:
                to = (y + r) % NY
                send(backs.at[up(d) * NY + to], incoming.at[slot], b_s.at[0], b_r.at[0], dev(dy=to, dz=up(d)))

    wait(arrived_end.at[pl.ds(0, NZ - 1)], e_r.at[0])
    grad = jnp.zeros((8, LANES), F32)
    for zz in range(NZ):
        grad = grad + arrived_end[zz] * ins[zz]
    grad = grad + pltpu.roll(grad, 4, 0)
    grad = (grad + pltpu.roll(grad, 2, 0))[:2]
    wait(inrow_in.at[pl.ds(0, NZ - 1)], i_r.at[0])
    for zz in range(NZ):
        grad = grad + inrow_in[zz]
    rowsum[...] = grad * F32(1.0 / LENGTH)
    rowsum_in[slot] = rowsum[...]
    for d in served:
        for r in (2, 1, 3, 0):
            if d or r:
                to = (y + r) % NY
                send(rowsum, rowsum_in.at[slot], t_s.at[0], t_r.at[0], dev(dy=to, dz=up(d)))

    wait(near.at[pl.ds(0, 3 * ROWS), :], n_r.at[0])
    wait(incoming.at[pl.ds(0, half_modes * NY - 1)], b_r.at[0])
    carried = [None] * MODES
    for p in range(half_modes):
        both = jnp.concatenate([incoming[p * NY + q] for q in range(NY)], axis=0)
        for m, late in (
            (p, jnp.where(even, both, next_down(both))),
            (p + half_modes, jnp.where(even, next_up(both), both)),
        ):
            carried[m] = jnp.where(even, seg_all[m] * late, late)

    def far_step(i, sums):
        t = SEG - 1 - i
        sums = tuple(dec_all[m] * s for m, s in enumerate(sums))
        acc = near[pl.ds(t, 8, stride=SEG), :]
        for m in range(MODES):
            acc = acc + resb_all[m] * sums[m]
        outf[pl.ds(t, 8, stride=SEG), :] = acc
        return sums

    lax.fori_loop(0, SEG, far_step, tuple(carried), unroll=UNROLL)
    for q in range(NY):
        out[:, q * LANES : (q + 1) * LANES] = outf[q * ROWS : (q + 1) * ROWS, :].astype(BF16)

    wait(rowsum_in.at[pl.ds(0, half_modes * NY - 1)], t_r.at[0])
    for m in range(MODES):
        for q in range(NY):
            j = m // half_modes
            rout[m : m + 1, q * LANES : (q + 1) * LANES] = rowsum_in[(m % half_modes) * NY + q, j : j + 1, :]

    wait(gobuf.at[pl.ds(0, 31)], go_s.at[0])
    wait(wbuf.at[pl.ds(0, 63)], z_s.at[0])
    wait(gtcv.at[pl.ds(0, 6)], gc_s.at[0])
    wait(arrived.at[pl.ds(0, NZ - 1)], a_s.at[0])
    wait(arrived.at[pl.ds(0, NZ - 1)], e_s.at[0])
    wait(inrow_in.at[pl.ds(0, NZ - 1)], i_s.at[0])
    wait(near.at[pl.ds(0, 3 * ROWS), :], n_s.at[0])
    wait(incoming.at[pl.ds(0, 31)], b_s.at[0])
    wait(incoming.at[pl.ds(0, 31)], t_s.at[0])


def local(grad_out, gate, conv_input, out_weight, residues, rates):
    hbm = pl.BlockSpec(memory_space=pltpu.HBM)
    vmem = pl.BlockSpec(memory_space=pltpu.VMEM)
    dma = pltpu.SemaphoreType.DMA

    def f32(*shape):
        return pltpu.VMEM(shape, F32)

    def bf16(*shape):
        return pltpu.VMEM(shape, BF16)

    operands = (grad_out, gate, conv_input, out_weight.T, residues, rates)
    operands = [pltpu.with_memory_space_constraint(a, pltpu.HBM) for a in operands]
    return pl.pallas_call(
        kernel,
        name="modal_backward",
        out_shape=(
            jax.ShapeDtypeStruct((ROWS, WIDE), BF16),
            jax.ShapeDtypeStruct((MODES, WIDE), F32),
        ),
        in_specs=[hbm] * 6,
        out_specs=(vmem, vmem),
        scratch_shapes=[
            bf16(2 * NX * NY, ROWS, WIDE),
            bf16(NY * NZ, 64, LANES),
            bf16(2 * NY, ROWS, LANES),
            f32(MODES, LANES),
            f32(MODES, LANES),
            f32(MODES, WIDE),
            f32(MODES, WIDE),
            f32(MODES, 8, LANES),
            f32(MODES, 8, LANES),
            f32(MODES, 8, LANES),
            f32(MODES, 8, LANES),
            f32(MODES, 8, LANES),
            f32(NY * ROWS, LANES),
            f32(NY * ROWS, LANES),
            f32(NY * ROWS, LANES),
            f32(NY * ROWS, LANES),
            f32(SEG, MODES, 8, LANES),
            f32(MODES, 8, LANES),
            f32(MODES // 2, 8, LANES),
            f32(NZ, 8, LANES),
            f32(MODES // 2, 8, LANES),
            f32(NZ, 8, LANES),
            f32(MODES // 2, 2, LANES),
            f32(NZ, 2, LANES),
            f32(NZ * NY, 2, LANES),
            f32(MODES // 2 * NY, 2, LANES),
            f32(2, LANES),
            f32(MODES // 2 * NY, 2, LANES),
            f32(NY * ROWS, LANES),
            dma((8,)),
            dma((1,)), dma((30,)), dma((1,)),
            dma((1,)), dma((24,)), dma((2,)), dma((4,)),
            dma((1,)), dma((1,)),
            dma((1,)), dma((1,)),
            dma((1,)), dma((1,)),
            dma((1,)), dma((1,)),
            dma((1,)), dma((1,)),
            dma((1,)), dma((1,)),
            dma((1,)), dma((1,)),
        ],
        compiler_params=pltpu.CompilerParams(
            collective_id=1, has_side_effects=True, vmem_limit_bytes=32 << 20
        ),
    )(*operands)


def solution(mesh):
    placed = (
        P("ctx", "tp"),
        P("ctx", "tp"),
        P("ctx", "tp"),
        P("tp", "ctx"),
        P(None, "tp"),
        P(None, "tp"),
    )
    return jax.shard_map(
        local,
        mesh=mesh,
        in_specs=placed,
        out_specs=(P("ctx", "tp"), P(None, "tp")),
        check_vma=False,
    )
```

```python
import jax
import jax.numpy as jnp
from jax import lax
from jax.experimental import pallas as pl
from jax.experimental.pallas import tpu as pltpu
from jax.sharding import PartitionSpec as P

MESH = pl.DeviceIdType.MESH
F32 = jnp.float32
BF16 = jnp.bfloat16
MODES = 16
NX = 4
NY = 4
NZ = 16
ROWS = 128
WIDE = 512
LANES = 128
SEG = 64
LENGTH = 8192
UNROLL = 4
HOPS = {0: (2, 1), 2: (2, 1), 4: (2, 1), 6: (2, 1)}


def kernel(
    go, gate, conv, weight, residues, rates,
    out, rout,
    gobuf, wbuf, gtcv, rt, rs, rt_all, rs_all,
    dec, resb, dec_all, resb_all, seg_all, gc, cvf, nearf, near, heads, ends, sent, arrived, sent_end, arrived_end,
    inrow, inrow_in, backs, incoming, rowsum, rowsum_in, outf,
    loc_sem, go_s, go_r, sib_r, z_s, z_r, leaf_r, y_r, gc_s, gc_r,
    a_s, a_r, e_s, e_r, i_s, i_r, n_s, n_r, b_s, b_r, t_s, t_r,
):
    ctx = lax.axis_index("ctx")
    tp = lax.axis_index("tp")
    x, k = tp // 2, tp % 2
    y, z = ctx // NZ, ctx % NZ
    xp, xm, x2 = (x + 1) % NX, (x + 3) % NX, (x + 2) % NX
    yp, ym, y2 = (y + 1) % NY, (y + 3) % NY, (y + 2) % NY

    def up(n):
        return (z + NZ + n) % NZ

    def dev(dx=None, dy=None, dz=None, dk=None):
        xx = x if dx is None else dx
        yy = y if dy is None else dy
        zz = z if dz is None else dz
        kk = k if dk is None else dk
        return (yy * NZ + zz, xx * 2 + kk)

    near_devices = [dev(dx=xp), dev(dx=xm), dev(dx=x2), dev(dk=1 - k)]
    near_devices += [dev(dz=up(n)) for n in (1, -1, 2, -2)]
    near_devices += [dev(dy=yy) for yy in (yp, ym, y2)]
    barrier = pltpu.get_barrier_semaphore()
    for d in near_devices:
        pl.semaphore_signal(barrier, inc=1, device_id=d, device_id_type=MESH)

    def send(src, dst, ss, rs_, target):
        pltpu.make_async_remote_copy(
            src_ref=src, dst_ref=dst, send_sem=ss, recv_sem=rs_, device_id=target, device_id_type=MESH
        ).start()

    def wait(ref, sem):
        pltpu.make_async_copy(ref, ref, sem).wait()

    def lanes(i):
        return pl.ds(pl.multiple_of(i * LANES, LANES), LANES)

    def shard(ox, core, oy):
        return (ox * 2 + core) * NY + oy

    def piece(r, owner):
        return r * NZ + owner

    cols = lanes(y)
    locals_ = [
        pltpu.make_async_copy(go, gobuf.at[shard(x, k, y)], loc_sem.at[0]),
        pltpu.make_async_copy(gate.at[:, cols], gtcv.at[y], loc_sem.at[1]),
        pltpu.make_async_copy(conv.at[:, cols], gtcv.at[NY + y], loc_sem.at[2]),
        pltpu.make_async_copy(rates.at[:, cols], rt, loc_sem.at[3]),
        pltpu.make_async_copy(residues.at[:, cols], rs, loc_sem.at[4]),
        pltpu.make_async_copy(weight.at[:, cols], wbuf.at[piece(0, z)], loc_sem.at[5]),
        pltpu.make_async_copy(rates, rt_all, loc_sem.at[6]),
        pltpu.make_async_copy(residues, rs_all, loc_sem.at[7]),
    ]
    for c in locals_:
        c.start()

    pl.semaphore_wait(barrier, len(near_devices))

    def z_slot(way, r, far):
        return (r * 2 + way) * 3 + far // 2 - 1

    def z_send(way, r, owner, far, hop, src=None, to=None):
        ref = wbuf.at[piece(r, owner)]
        target = dev(dy=to, dz=up(-hop if way else hop))
        if far in HOPS:
            sem = z_r.at[z_slot(way, r, far)]
        else:
            sem = leaf_r.at[0 if far < 6 else 1]
        send(ref if src is None else src, ref, z_s.at[0], sem, target)

    def z_wait(way, r, far):
        wait(wbuf.at[piece(r, up(far if way else -far))], z_r.at[z_slot(way, r, far)])

    for r in (0, 1, 3, 2):
        to = (y + NY - r) % NY
        src = weight.at[:, lanes(to)]
        for hop in HOPS[0] if r == 0 else ():
            for way in (0, 1):
                z_send(way, r, z, hop, hop, src, to)
    for r in (1, 3, 2):
        to = (y + NY - r) % NY
        send(weight.at[:, lanes(to)], wbuf.at[piece(r, z)], z_s.at[0], y_r.at[r], dev(dy=to))

    A, B = (0, 48), (48, 80)
    A0, A1, B0, B1 = (0, 32), (32, 16), (48, 48), (96, 32)
    go_slots = {}

    def go_ref(ox, oy, part):
        return gobuf.at[shard(ox, k, oy), pl.ds(part[0], part[1]), :]

    def go_send(key, ox, oy, part, target, src=None):
        slot = go_slots.setdefault(key, len(go_slots))
        ref = go_ref(ox, oy, part)
        send(ref if src is None else src, ref, go_s.at[0], go_r.at[slot], target)

    def go_wait(key, ox, oy, part):
        wait(go_ref(ox, oy, part), go_r.at[go_slots[key]])

    one_way = (("L", dev(dx=xp)), ("R", dev(dx=xm)), ("X2", dev(dx=x2)))
    other_way = (("D", dev(dy=yp)), ("U", dev(dy=ym)), ("Y2", dev(dy=y2)))
    for near_part, far_part in ((A, B), (B, A)):
        for way, part in ((one_way, near_part), (other_way, far_part)):
            for key, target in way:
                go_send((key, part), x, y, part, target, go.at[pl.ds(part[0], part[1]), :])

    sib_slots = []

    def sibling(ox, oy, src=None):
        ref = gobuf.at[shard(ox, k, oy)]
        send(ref if src is None else src, ref, go_s.at[0], sib_r.at[0], dev(dk=1 - k))
        sib_slots.append((ox, oy))

    sibling(x, y, go)

    def z_round(far, pieces=(0, 1, 3, 2)):
        for r in pieces:
            for way in (0, 1):
                owner = up(far if way else -far)
                z_wait(way, r, far)
                for hop in HOPS[far]:
                    if far + hop < 8 or way == r % 2:
                        z_send(way, r, owner, far + hop, hop)

    def y_pieces():
        for r in (1, 3, 2):
            wait(wbuf.at[piece(r, z)], y_r.at[r])
            for hop in HOPS[0]:
                for way in (0, 1):
                    z_send(way, r, z, hop, hop)

    columns = (("L", xm), ("R", xp), ("X2", x2))
    lines_ = (("D", ym), ("U", yp), ("Y2", y2))

    def turn(i):
        key, ox = columns[i]
        go_wait((key, A), ox, y, A)
        go_send((key, "D"), ox, y, A, dev(dy=yp))
        go_send((key, "U"), ox, y, A, dev(dy=ym))
        key, oy = lines_[i]
        go_wait((key, B), x, oy, B)
        go_send((key, "L"), x, oy, B, dev(dx=xp))
        go_send((key, "R"), x, oy, B, dev(dx=xm))

    def onward(i):
        key, ox = columns[i]
        go_wait((key, "D"), ox, ym, A)
        go_send((key, "Y2"), ox, ym, A0, dev(dy=yp))
        go_wait((key, "U"), ox, yp, A)
        go_send((key, "Y2"), ox, yp, A1, dev(dy=ym))
        key, oy = lines_[i]
        go_wait((key, "L"), xm, oy, B)
        go_send((key, "X2"), xm, oy, B0, dev(dx=xp))
        go_wait((key, "R"), xp, oy, B)
        go_send((key, "X2"), xp, oy, B1, dev(dx=xm))

    def gates():
        for r in range(1, NY):
            to = (y + r) % NY
            send(gate.at[:, lanes(to)], gtcv.at[y], gc_s.at[0], gc_r.at[0], dev(dy=to))
            send(conv.at[:, lanes(to)], gtcv.at[NY + y], gc_s.at[0], gc_r.at[0], dev(dy=to))

    def near_shards(i):
        key, ox = columns[i]
        go_wait((key, B), ox, y, B)
        sibling(ox, y)
        key, oy = lines_[i]
        go_wait((key, A), x, oy, A)
        sibling(x, oy)

    def diagonal_shards():
        for ox in (xm, xp):
            for oy in (ym, yp):
                sibling(ox, oy)

    def far_shards(i):
        key, ox = columns[i]
        go_wait((key, "Y2"), ox, y2, A)
        if i < 2:
            sibling(ox, y2)
        key, oy = lines_[i]
        go_wait((key, "X2"), x2, oy, B)
        sibling(x2, oy)

    def spread(ref, m):
        rows = [jnp.broadcast_to(ref[m : m + 1, q * LANES : (q + 1) * LANES], (2, LANES)) for q in range(NY)]
        return jnp.concatenate(rows, axis=0)

    def decays():
        for c in locals_:
            c.wait()
        for m in range(MODES):
            dec[m] = jnp.broadcast_to(jnp.exp(-rt[m : m + 1, :]), (8, LANES))
            resb[m] = jnp.broadcast_to(rs[m : m + 1, :], (8, LANES))
            rate = spread(rt_all, m)
            dec_all[m] = jnp.exp(-rate)
            seg_all[m] = jnp.exp(-rate * F32(SEG))
            resb_all[m] = spread(rs_all, m)

    row = lax.broadcasted_iota(jnp.int32, (8, LANES), 0)
    even = row % 2 == 0

    def by_seg(m):
        return jnp.broadcast_to(jnp.exp(-rt[m : m + 1, :] * F32(SEG)), (8, LANES))

    def next_up(v):
        return pltpu.roll(v, 7, 0)

    def next_down(v):
        return pltpu.roll(v, 1, 0)

    half_modes = MODES // 2
    far_first = [8]
    for d in range(7, 0, -1):
        far_first += [d, -d]

    zeros = tuple(jnp.zeros((8, LANES), F32) for _ in range(MODES))

    def head_step(t, sums):
        c = cvf[pl.ds(t, 8, stride=SEG), :]
        sums = tuple(dec[m] * s + c for m, s in enumerate(sums))
        for m, s in enumerate(sums):
            heads[t, m] = s
        return sums

    def input_ends():
        wait(gtcv.at[pl.ds(0, 6)], gc_r.at[0])
        cvf[...] = gtcv[NY : 2 * NY].reshape(NY * ROWS, LANES).astype(F32)
        sums = lax.fori_loop(0, SEG, head_step, zeros)
        sums = [dec[m] * s for m, s in enumerate(sums)]
        for m, s in enumerate(sums):
            ends[m] = s
        for p in range(half_modes):
            s, o = sums[p], sums[p + half_modes]
            sent_end[p] = jnp.where(even, next_up(s) + by_seg(p) * s, o + by_seg(p + half_modes) * next_down(o))
        arrived_end[z] = sent_end[z % half_modes]

    def send_ends(chips):
        for d in chips:
            send(sent_end.at[up(d) % half_modes], arrived_end.at[z], e_s.at[0], e_r.at[0], dev(dz=up(d)))

    def z_leaves(group):
        wait(wbuf.at[pl.ds(0, 24 if group == 0 else 12)], leaf_r.at[group])

    y_pieces()
    z_round(2, (0,))
    turn(0)
    turn(1)
    z_round(2, (1, 3, 2))
    turn(2)
    decays()
    near_shards(0)
    near_shards(1)
    near_shards(2)
    gates()
    z_round(4, (0, 1))
    onward(0)
    z_round(4, (3, 2))
    onward(1)
    diagonal_shards()
    onward(2)
    input_ends()
    z_round(6, (0, 1))
    far_shards(0)
    z_round(6, (3, 2))
    z_leaves(0)
    send_ends((6, -6, 5, -5, 4, -4, 3, -3, 2, -2, 1, -1))
    far_shards(1)
    far_shards(2)
    z_leaves(1)
    send_ends((8, 7, -7))
    wait(gobuf.at[pl.ds(0, NX * NY)], sib_r.at[0])

    total = jnp.zeros((NY * ROWS, LANES), F32)
    for ox in range(NX):
        rel = (ox + NY - y) % NY
        for half in range(2):
            a = gobuf[(ox * 2 + half) * NY : (ox * 2 + half + 1) * NY].reshape(NY * ROWS, WIDE)
            w = wbuf[pl.ds(rel * NZ + half * 8, 8)].reshape(WIDE, LANES)
            total = total + jnp.dot(a, w, preferred_element_type=F32)
    gc[...] = total * gtcv[:NY].reshape(NY * ROWS, LANES).astype(F32)

    def start_step(i, sums):
        g = gc[pl.ds(SEG - 1 - i, 8, stride=SEG), :]
        return tuple(dec[m] * s + g for m, s in enumerate(sums))

    sums = lax.fori_loop(0, SEG, start_step, zeros, unroll=UNROLL)
    for p in range(half_modes):
        s, o = sums[p], sums[p + half_modes]
        sent[p] = jnp.where(even, s + by_seg(p) * next_up(s), next_down(o) + by_seg(p + half_modes) * o)

    arrived[z] = sent[z % half_modes]
    for d in far_first:
        send(sent.at[up(d) % half_modes], arrived.at[z], a_s.at[0], a_r.at[0], dev(dz=up(d)))
    def inner_step(t, inner):
        g = gc[pl.ds(t, 8, stride=SEG), :]
        return tuple(n + g * heads[t, m] for m, n in enumerate(inner))

    inner = lax.fori_loop(0, SEG, inner_step, zeros, unroll=UNROLL)
    from_second = tuple(jnp.where(even, next_up(s), 0.0) for s in sums)
    inner = [n + ends[m] * s for m, (n, s) in enumerate(zip(inner, from_second))]
    for m in range(MODES):
        inrow[m % half_modes, m // half_modes : m // half_modes + 1, :] = jnp.sum(inner[m], axis=0, keepdims=True)
    inrow_in[z] = inrow[z % half_modes]
    for d in far_first:
        send(inrow.at[up(d) % half_modes], inrow_in.at[z], i_s.at[0], i_r.at[0], dev(dz=up(d)))

    def near_step(i, sums):
        t = SEG - 1 - i
        g = gc[pl.ds(t, 8, stride=SEG), :]
        sums = tuple(dec[m] * s + g for m, s in enumerate(sums))
        acc = resb[0] * sums[0]
        for m in range(1, MODES):
            acc = acc + resb[m] * sums[m]
        nearf[pl.ds(t, 8, stride=SEG), :] = acc
        return sums

    lax.fori_loop(0, SEG, near_step, from_second, unroll=UNROLL)
    for r in (2, 1, 3):
        to = (y + r) % NY
        rows = pl.ds(pl.multiple_of(to * ROWS, ROWS), ROWS)
        mine = pl.ds(pl.multiple_of(y * ROWS, ROWS), ROWS)
        send(nearf.at[rows, :], near.at[mine, :], n_s.at[0], n_r.at[0], dev(dy=to))
    near[mine, :] = nearf[mine, :]

    pair = z % half_modes
    rate = jnp.where(even, rt[pl.ds(pair, 1), :], rt[pl.ds(pair + half_modes, 1), :])
    by_block = jnp.exp(-rate * F32(ROWS))
    by_line = jnp.exp(-rate * F32(ROWS * NZ))
    to_line = [jnp.exp(-rate * F32(ROWS * (NZ - 1 - zz))) for zz in range(NZ)]
    wait(arrived.at[pl.ds(0, NZ - 1)], a_r.at[0])
    after = [None] * NZ
    after[NZ - 1] = jnp.zeros((8, LANES), F32)
    for zz in range(NZ - 2, -1, -1):
        after[zz] = arrived[zz + 1] + by_block * after[zz + 1]
    line = arrived[0] + by_block * after[0]

    def next_line(v):
        return jnp.where(row < 6, pltpu.roll(v, 6, 0), 0.0)

    line_next = next_line(line)
    lines = line_next
    for _ in range(NY - 2):
        lines = line_next + by_line * next_line(lines)
    ins = []
    for zz in range(NZ):
        ins.append(after[zz] + to_line[zz] * lines)
        for b in range(NY):
            backs[zz * NY + b] = ins[zz][2 * b : 2 * b + 2]

    served = (-4, 3, -3, 2, -2, 1, -1, 0)
    slot = pair * NY + y
    incoming[slot] = backs[z * NY + y]
    for d in served:
        for r in (2, 1, 3, 0):
            if d or r:
                to = (y + r) % NY
                send(backs.at[up(d) * NY + to], incoming.at[slot], b_s.at[0], b_r.at[0], dev(dy=to, dz=up(d)))

    wait(arrived_end.at[pl.ds(0, NZ - 1)], e_r.at[0])
    grad = jnp.zeros((8, LANES), F32)
    for zz in range(NZ):
        grad = grad + arrived_end[zz] * ins[zz]
    grad = grad + pltpu.roll(grad, 4, 0)
    grad = (grad + pltpu.roll(grad, 2, 0))[:2]
    wait(inrow_in.at[pl.ds(0, NZ - 1)], i_r.at[0])
    for zz in range(NZ):
        grad = grad + inrow_in[zz]
    rowsum[...] = grad * F32(1.0 / LENGTH)
    rowsum_in[slot] = rowsum[...]
    for d in served:
        for r in (2, 1, 3, 0):
            if d or r:
                to = (y + r) % NY
                send(rowsum, rowsum_in.at[slot], t_s.at[0], t_r.at[0], dev(dy=to, dz=up(d)))

    wait(near.at[pl.ds(0, 3 * ROWS), :], n_r.at[0])
    wait(incoming.at[pl.ds(0, half_modes * NY - 1)], b_r.at[0])
    carried = [None] * MODES
    for p in range(half_modes):
        both = jnp.concatenate([incoming[p * NY + q] for q in range(NY)], axis=0)
        for m, late in (
            (p, jnp.where(even, both, next_down(both))),
            (p + half_modes, jnp.where(even, next_up(both), both)),
        ):
            carried[m] = jnp.where(even, seg_all[m] * late, late)

    def far_step(i, sums):
        t = SEG - 1 - i
        sums = tuple(dec_all[m] * s for m, s in enumerate(sums))
        acc = near[pl.ds(t, 8, stride=SEG), :]
        for m in range(MODES):
            acc = acc + resb_all[m] * sums[m]
        outf[pl.ds(t, 8, stride=SEG), :] = acc
        return sums

    lax.fori_loop(0, SEG, far_step, tuple(carried), unroll=UNROLL)
    for q in range(NY):
        out[:, q * LANES : (q + 1) * LANES] = outf[q * ROWS : (q + 1) * ROWS, :].astype(BF16)

    wait(rowsum_in.at[pl.ds(0, half_modes * NY - 1)], t_r.at[0])
    for m in range(MODES):
        for q in range(NY):
            j = m // half_modes
            rout[m : m + 1, q * LANES : (q + 1) * LANES] = rowsum_in[(m % half_modes) * NY + q, j : j + 1, :]

    wait(gobuf.at[pl.ds(0, 31)], go_s.at[0])
    wait(wbuf.at[pl.ds(0, 63)], z_s.at[0])
    wait(gtcv.at[pl.ds(0, 6)], gc_s.at[0])
    wait(arrived.at[pl.ds(0, NZ - 1)], a_s.at[0])
    wait(arrived.at[pl.ds(0, NZ - 1)], e_s.at[0])
    wait(inrow_in.at[pl.ds(0, NZ - 1)], i_s.at[0])
    wait(near.at[pl.ds(0, 3 * ROWS), :], n_s.at[0])
    wait(incoming.at[pl.ds(0, 31)], b_s.at[0])
    wait(incoming.at[pl.ds(0, 31)], t_s.at[0])


def local(grad_out, gate, conv_input, out_weight, residues, rates):
    hbm = pl.BlockSpec(memory_space=pltpu.HBM)
    vmem = pl.BlockSpec(memory_space=pltpu.VMEM)
    dma = pltpu.SemaphoreType.DMA

    def f32(*shape):
        return pltpu.VMEM(shape, F32)

    def bf16(*shape):
        return pltpu.VMEM(shape, BF16)

    operands = (grad_out, gate, conv_input, out_weight.T, residues, rates)
    operands = [pltpu.with_memory_space_constraint(a, pltpu.HBM) for a in operands]
    return pl.pallas_call(
        kernel,
        name="modal_backward",
        out_shape=(
            jax.ShapeDtypeStruct((ROWS, WIDE), BF16),
            jax.ShapeDtypeStruct((MODES, WIDE), F32),
        ),
        in_specs=[hbm] * 6,
        out_specs=(vmem, vmem),
        scratch_shapes=[
            bf16(2 * NX * NY, ROWS, WIDE),
            bf16(NY * NZ, 64, LANES),
            bf16(2 * NY, ROWS, LANES),
            f32(MODES, LANES),
            f32(MODES, LANES),
            f32(MODES, WIDE),
            f32(MODES, WIDE),
            f32(MODES, 8, LANES),
            f32(MODES, 8, LANES),
            f32(MODES, 8, LANES),
            f32(MODES, 8, LANES),
            f32(MODES, 8, LANES),
            f32(NY * ROWS, LANES),
            f32(NY * ROWS, LANES),
            f32(NY * ROWS, LANES),
            f32(NY * ROWS, LANES),
            f32(SEG, MODES, 8, LANES),
            f32(MODES, 8, LANES),
            f32(MODES // 2, 8, LANES),
            f32(NZ, 8, LANES),
            f32(MODES // 2, 8, LANES),
            f32(NZ, 8, LANES),
            f32(MODES // 2, 2, LANES),
            f32(NZ, 2, LANES),
            f32(NZ * NY, 2, LANES),
            f32(MODES // 2 * NY, 2, LANES),
            f32(2, LANES),
            f32(MODES // 2 * NY, 2, LANES),
            f32(NY * ROWS, LANES),
            dma((8,)),
            dma((1,)), dma((30,)), dma((1,)),
            dma((1,)), dma((24,)), dma((2,)), dma((4,)),
            dma((1,)), dma((1,)),
            dma((1,)), dma((1,)),
            dma((1,)), dma((1,)),
            dma((1,)), dma((1,)),
            dma((1,)), dma((1,)),
            dma((1,)), dma((1,)),
            dma((1,)), dma((1,)),
        ],
        compiler_params=pltpu.CompilerParams(
            collective_id=1, has_side_effects=True, vmem_limit_bytes=32 << 20
        ),
    )(*operands)


def solution(mesh):
    placed = (
        P("ctx", "tp"),
        P("ctx", "tp"),
        P("ctx", "tp"),
        P("tp", "ctx"),
        P(None, "tp"),
        P(None, "tp"),
    )
    return jax.shard_map(
        local,
        mesh=mesh,
        in_specs=placed,
        out_specs=(P("ctx", "tp"), P(None, "tp")),
        check_vma=False,
    )
```

```python
import jax
import jax.numpy as jnp
from jax import lax
from jax.experimental import pallas as pl
from jax.experimental.pallas import tpu as pltpu
from jax.sharding import PartitionSpec as P

MESH = pl.DeviceIdType.MESH
F32 = jnp.float32
BF16 = jnp.bfloat16
MODES = 16
NX = 4
NY = 4
NZ = 16
ROWS = 128
WIDE = 512
LANES = 128
SEG = 64
LENGTH = 8192
UNROLL = 4
HOPS = {0: (2, 1), 2: (2, 1), 4: (2, 1), 6: (2, 1)}


def kernel(
    go, gate, conv, weight, residues, rates,
    out, rout,
    gobuf, wbuf, gtcv, rt, rs, rt_all, rs_all,
    dec, resb, dec_all, resb_all, seg_all, gc, cvf, nearf, near, heads, ends, sent, arrived, sent_end, arrived_end,
    inrow, inrow_in, backs, late_all, incoming, rowsum, rowsum_in, outf,
    loc_sem, go_s, go_r, sib_r, z_s, z_r, leaf_r, y_r, gc_s, gc_r,
    a_s, a_r, e_s, e_r, i_s, i_r, n_s, n_r, b_s, b_r, t_s, t_r,
):
    ctx = lax.axis_index("ctx")
    tp = lax.axis_index("tp")
    x, k = tp // 2, tp % 2
    y, z = ctx // NZ, ctx % NZ
    xp, xm, x2 = (x + 1) % NX, (x + 3) % NX, (x + 2) % NX
    yp, ym, y2 = (y + 1) % NY, (y + 3) % NY, (y + 2) % NY

    def up(n):
        return (z + NZ + n) % NZ

    def dev(dx=None, dy=None, dz=None, dk=None):
        xx = x if dx is None else dx
        yy = y if dy is None else dy
        zz = z if dz is None else dz
        kk = k if dk is None else dk
        return (yy * NZ + zz, xx * 2 + kk)

    near_devices = [dev(dx=xp), dev(dx=xm), dev(dx=x2), dev(dk=1 - k)]
    near_devices += [dev(dz=up(n)) for n in (1, -1, 2, -2)]
    near_devices += [dev(dy=yy) for yy in (yp, ym, y2)]
    barrier = pltpu.get_barrier_semaphore()
    for d in near_devices:
        pl.semaphore_signal(barrier, inc=1, device_id=d, device_id_type=MESH)

    def send(src, dst, ss, rs_, target):
        pltpu.make_async_remote_copy(
            src_ref=src, dst_ref=dst, send_sem=ss, recv_sem=rs_, device_id=target, device_id_type=MESH
        ).start()

    def wait(ref, sem):
        pltpu.make_async_copy(ref, ref, sem).wait()

    def lanes(i):
        return pl.ds(pl.multiple_of(i * LANES, LANES), LANES)

    def shard(ox, core, oy):
        return (ox * 2 + core) * NY + oy

    def piece(r, owner):
        return r * NZ + owner

    cols = lanes(y)
    locals_ = [
        pltpu.make_async_copy(go, gobuf.at[shard(x, k, y)], loc_sem.at[0]),
        pltpu.make_async_copy(gate.at[:, cols], gtcv.at[y], loc_sem.at[1]),
        pltpu.make_async_copy(conv.at[:, cols], gtcv.at[NY + y], loc_sem.at[2]),
        pltpu.make_async_copy(rates.at[:, cols], rt, loc_sem.at[3]),
        pltpu.make_async_copy(residues.at[:, cols], rs, loc_sem.at[4]),
        pltpu.make_async_copy(weight.at[:, cols], wbuf.at[piece(0, z)], loc_sem.at[5]),
        pltpu.make_async_copy(rates, rt_all, loc_sem.at[6]),
        pltpu.make_async_copy(residues, rs_all, loc_sem.at[7]),
    ]
    for c in locals_:
        c.start()

    pl.semaphore_wait(barrier, len(near_devices))

    def z_slot(way, r, far):
        return (r * 2 + way) * 3 + far // 2 - 1

    def z_send(way, r, owner, far, hop, src=None, to=None):
        ref = wbuf.at[piece(r, owner)]
        target = dev(dy=to, dz=up(-hop if way else hop))
        if far in HOPS:
            sem = z_r.at[z_slot(way, r, far)]
        else:
            sem = leaf_r.at[0 if far < 6 else 1]
        send(ref if src is None else src, ref, z_s.at[0], sem, target)

    def z_wait(way, r, far):
        wait(wbuf.at[piece(r, up(far if way else -far))], z_r.at[z_slot(way, r, far)])

    for r in (0, 1, 3, 2):
        to = (y + NY - r) % NY
        src = weight.at[:, lanes(to)]
        for hop in HOPS[0] if r == 0 else ():
            for way in (0, 1):
                z_send(way, r, z, hop, hop, src, to)
    for r in (1, 3, 2):
        to = (y + NY - r) % NY
        send(weight.at[:, lanes(to)], wbuf.at[piece(r, z)], z_s.at[0], y_r.at[r], dev(dy=to))

    A, B = (0, 48), (48, 80)
    A0, A1, B0, B1 = (0, 32), (32, 16), (48, 48), (96, 32)
    go_slots = {}

    def go_ref(ox, oy, part):
        return gobuf.at[shard(ox, k, oy), pl.ds(part[0], part[1]), :]

    def go_send(key, ox, oy, part, target, src=None):
        slot = go_slots.setdefault(key, len(go_slots))
        ref = go_ref(ox, oy, part)
        send(ref if src is None else src, ref, go_s.at[0], go_r.at[slot], target)

    def go_wait(key, ox, oy, part):
        wait(go_ref(ox, oy, part), go_r.at[go_slots[key]])

    one_way = (("L", dev(dx=xp)), ("R", dev(dx=xm)), ("X2", dev(dx=x2)))
    other_way = (("D", dev(dy=yp)), ("U", dev(dy=ym)), ("Y2", dev(dy=y2)))
    for near_part, far_part in ((A, B), (B, A)):
        for way, part in ((one_way, near_part), (other_way, far_part)):
            for key, target in way:
                go_send((key, part), x, y, part, target, go.at[pl.ds(part[0], part[1]), :])

    sib_slots = []

    def sibling(ox, oy, src=None):
        ref = gobuf.at[shard(ox, k, oy)]
        send(ref if src is None else src, ref, go_s.at[0], sib_r.at[0], dev(dk=1 - k))
        sib_slots.append((ox, oy))

    sibling(x, y, go)

    def z_round(far, pieces=(0, 1, 3, 2)):
        for r in pieces:
            for way in (0, 1):
                owner = up(far if way else -far)
                z_wait(way, r, far)
                for hop in HOPS[far]:
                    if far + hop < 8 or way == r % 2:
                        z_send(way, r, owner, far + hop, hop)

    def y_pieces():
        for r in (1, 3, 2):
            wait(wbuf.at[piece(r, z)], y_r.at[r])
            for hop in HOPS[0]:
                for way in (0, 1):
                    z_send(way, r, z, hop, hop)

    columns = (("L", xm), ("R", xp), ("X2", x2))
    lines_ = (("D", ym), ("U", yp), ("Y2", y2))

    def turn(i):
        key, ox = columns[i]
        go_wait((key, A), ox, y, A)
        go_send((key, "D"), ox, y, A, dev(dy=yp))
        go_send((key, "U"), ox, y, A, dev(dy=ym))
        key, oy = lines_[i]
        go_wait((key, B), x, oy, B)
        go_send((key, "L"), x, oy, B, dev(dx=xp))
        go_send((key, "R"), x, oy, B, dev(dx=xm))

    def onward(i):
        key, ox = columns[i]
        go_wait((key, "D"), ox, ym, A)
        go_send((key, "Y2"), ox, ym, A0, dev(dy=yp))
        go_wait((key, "U"), ox, yp, A)
        go_send((key, "Y2"), ox, yp, A1, dev(dy=ym))
        key, oy = lines_[i]
        go_wait((key, "L"), xm, oy, B)
        go_send((key, "X2"), xm, oy, B0, dev(dx=xp))
        go_wait((key, "R"), xp, oy, B)
        go_send((key, "X2"), xp, oy, B1, dev(dx=xm))

    def gates():
        for r in range(1, NY):
            to = (y + r) % NY
            send(gate.at[:, lanes(to)], gtcv.at[y], gc_s.at[0], gc_r.at[0], dev(dy=to))
            send(conv.at[:, lanes(to)], gtcv.at[NY + y], gc_s.at[0], gc_r.at[0], dev(dy=to))

    def near_shards(i):
        key, ox = columns[i]
        go_wait((key, B), ox, y, B)
        sibling(ox, y)
        key, oy = lines_[i]
        go_wait((key, A), x, oy, A)
        sibling(x, oy)

    def diagonal_shards():
        for ox in (xm, xp):
            for oy in (ym, yp):
                sibling(ox, oy)

    def far_shards(i):
        key, ox = columns[i]
        go_wait((key, "Y2"), ox, y2, A)
        if i < 2:
            sibling(ox, y2)
        key, oy = lines_[i]
        go_wait((key, "X2"), x2, oy, B)
        sibling(x2, oy)

    def spread(ref, m):
        rows = [jnp.broadcast_to(ref[m : m + 1, q * LANES : (q + 1) * LANES], (2, LANES)) for q in range(NY)]
        return jnp.concatenate(rows, axis=0)

    def decays():
        for c in locals_:
            c.wait()
        for m in range(MODES):
            dec[m] = jnp.broadcast_to(jnp.exp(-rt[m : m + 1, :]), (8, LANES))
            resb[m] = jnp.broadcast_to(rs[m : m + 1, :], (8, LANES))
            rate = spread(rt_all, m)
            dec_all[m] = jnp.exp(-rate)
            seg_all[m] = jnp.exp(-rate * F32(SEG))
            resb_all[m] = spread(rs_all, m)

    row = lax.broadcasted_iota(jnp.int32, (8, LANES), 0)
    even = row % 2 == 0

    def by_seg(m):
        return jnp.broadcast_to(jnp.exp(-rt[m : m + 1, :] * F32(SEG)), (8, LANES))

    def next_up(v):
        return pltpu.roll(v, 7, 0)

    def next_down(v):
        return pltpu.roll(v, 1, 0)

    half_modes = MODES // 2
    far_first = [8]
    for d in range(7, 0, -1):
        far_first += [d, -d]

    zeros = tuple(jnp.zeros((8, LANES), F32) for _ in range(MODES))

    def head_step(t, sums):
        c = cvf[pl.ds(t, 8, stride=SEG), :]
        sums = tuple(dec[m] * s + c for m, s in enumerate(sums))
        for m, s in enumerate(sums):
            heads[t, m] = s
        return sums

    def input_ends():
        wait(gtcv.at[pl.ds(0, 6)], gc_r.at[0])
        cvf[...] = gtcv[NY : 2 * NY].reshape(NY * ROWS, LANES).astype(F32)
        sums = lax.fori_loop(0, SEG, head_step, zeros)
        sums = [dec[m] * s for m, s in enumerate(sums)]
        for m, s in enumerate(sums):
            ends[m] = s
        for p in range(half_modes):
            s, o = sums[p], sums[p + half_modes]
            sent_end[p] = jnp.where(even, next_up(s) + by_seg(p) * s, o + by_seg(p + half_modes) * next_down(o))
        arrived_end[z] = sent_end[z % half_modes]

    def send_ends(chips):
        for d in chips:
            send(sent_end.at[up(d) % half_modes], arrived_end.at[z], e_s.at[0], e_r.at[0], dev(dz=up(d)))

    def z_leaves(group):
        wait(wbuf.at[pl.ds(0, 24 if group == 0 else 12)], leaf_r.at[group])

    y_pieces()
    z_round(2, (0,))
    turn(0)
    turn(1)
    z_round(2, (1, 3, 2))
    turn(2)
    decays()
    near_shards(0)
    near_shards(1)
    near_shards(2)
    gates()
    z_round(4, (0, 1))
    onward(0)
    z_round(4, (3, 2))
    onward(1)
    diagonal_shards()
    onward(2)
    z_round(6, (0, 1))
    input_ends()
    far_shards(0)
    z_round(6, (3, 2))
    z_leaves(0)
    send_ends((6, -6, 5, -5, 4, -4, 3, -3, 2, -2, 1, -1))
    far_shards(1)
    far_shards(2)
    z_leaves(1)
    send_ends((8, 7, -7))
    wait(gobuf.at[pl.ds(0, NX * NY)], sib_r.at[0])

    total = jnp.zeros((NY * ROWS, LANES), F32)
    for ox in range(NX):
        rel = (ox + NY - y) % NY
        for half in range(2):
            a = gobuf[(ox * 2 + half) * NY : (ox * 2 + half + 1) * NY].reshape(NY * ROWS, WIDE)
            w = wbuf[pl.ds(rel * NZ + half * 8, 8)].reshape(WIDE, LANES)
            total = total + jnp.dot(a, w, preferred_element_type=F32)
    gc[...] = total * gtcv[:NY].reshape(NY * ROWS, LANES).astype(F32)

    def start_step(i, sums):
        g = gc[pl.ds(SEG - 1 - i, 8, stride=SEG), :]
        return tuple(dec[m] * s + g for m, s in enumerate(sums))

    sums = lax.fori_loop(0, SEG, start_step, zeros, unroll=UNROLL)
    for p in range(half_modes):
        s, o = sums[p], sums[p + half_modes]
        sent[p] = jnp.where(even, s + by_seg(p) * next_up(s), next_down(o) + by_seg(p + half_modes) * o)

    arrived[z] = sent[z % half_modes]
    for d in far_first:
        send(sent.at[up(d) % half_modes], arrived.at[z], a_s.at[0], a_r.at[0], dev(dz=up(d)))
    def inner_step(t, inner):
        g = gc[pl.ds(t, 8, stride=SEG), :]
        return tuple(n + g * heads[t, m] for m, n in enumerate(inner))

    inner = lax.fori_loop(0, SEG, inner_step, zeros, unroll=UNROLL)
    from_second = tuple(jnp.where(even, next_up(s), 0.0) for s in sums)
    inner = [n + ends[m] * s for m, (n, s) in enumerate(zip(inner, from_second))]
    for m in range(MODES):
        inrow[m % half_modes, m // half_modes : m // half_modes + 1, :] = jnp.sum(inner[m], axis=0, keepdims=True)
    inrow_in[z] = inrow[z % half_modes]
    for d in far_first:
        send(inrow.at[up(d) % half_modes], inrow_in.at[z], i_s.at[0], i_r.at[0], dev(dz=up(d)))

    def near_step(i, sums):
        t = SEG - 1 - i
        g = gc[pl.ds(t, 8, stride=SEG), :]
        sums = tuple(dec[m] * s + g for m, s in enumerate(sums))
        acc = resb[0] * sums[0]
        for m in range(1, MODES):
            acc = acc + resb[m] * sums[m]
        nearf[pl.ds(t, 8, stride=SEG), :] = acc
        return sums

    lax.fori_loop(0, SEG, near_step, from_second, unroll=UNROLL)
    for r in (2, 1, 3):
        to = (y + r) % NY
        rows = pl.ds(pl.multiple_of(to * ROWS, ROWS), ROWS)
        mine = pl.ds(pl.multiple_of(y * ROWS, ROWS), ROWS)
        send(nearf.at[rows, :], near.at[mine, :], n_s.at[0], n_r.at[0], dev(dy=to))
    near[mine, :] = nearf[mine, :]

    pair = z % half_modes
    rate = jnp.where(even, rt[pl.ds(pair, 1), :], rt[pl.ds(pair + half_modes, 1), :])
    by_block = jnp.exp(-rate * F32(ROWS))
    by_line = jnp.exp(-rate * F32(ROWS * NZ))
    to_line = [jnp.exp(-rate * F32(ROWS * (NZ - 1 - zz))) for zz in range(NZ)]
    wait(arrived.at[pl.ds(0, NZ - 1)], a_r.at[0])
    after = [None] * NZ
    after[NZ - 1] = jnp.zeros((8, LANES), F32)
    for zz in range(NZ - 2, -1, -1):
        after[zz] = arrived[zz + 1] + by_block * after[zz + 1]
    line = arrived[0] + by_block * after[0]

    def next_line(v):
        return jnp.where(row < 6, pltpu.roll(v, 6, 0), 0.0)

    line_next = next_line(line)
    lines = line_next
    for _ in range(NY - 2):
        lines = line_next + by_line * next_line(lines)
    ins = []
    for zz in range(NZ):
        ins.append(after[zz] + to_line[zz] * lines)
        late_all[zz] = ins[zz]

    served = (-4, 3, -3, 2, -2, 1, -1, 0)
    slot = pair * NY + y
    for i, d in enumerate(served):
        late = late_all[up(d)]
        for b in range(NY):
            backs[i * NY + b] = late[2 * b : 2 * b + 2]
        if d == 0:
            incoming[slot] = backs[i * NY + y]
        for r in (2, 1, 3, 0):
            if d or r:
                to = (y + r) % NY
                send(backs.at[i * NY + to], incoming.at[slot], b_s.at[0], b_r.at[0], dev(dy=to, dz=up(d)))

    wait(arrived_end.at[pl.ds(0, NZ - 1)], e_r.at[0])
    grad = jnp.zeros((8, LANES), F32)
    for zz in range(NZ):
        grad = grad + arrived_end[zz] * ins[zz]
    grad = grad + pltpu.roll(grad, 4, 0)
    grad = (grad + pltpu.roll(grad, 2, 0))[:2]
    wait(inrow_in.at[pl.ds(0, NZ - 1)], i_r.at[0])
    for zz in range(NZ):
        grad = grad + inrow_in[zz]
    rowsum[...] = grad * F32(1.0 / LENGTH)
    rowsum_in[slot] = rowsum[...]
    for d in served:
        for r in (2, 1, 3, 0):
            if d or r:
                to = (y + r) % NY
                send(rowsum, rowsum_in.at[slot], t_s.at[0], t_r.at[0], dev(dy=to, dz=up(d)))

    wait(near.at[pl.ds(0, 3 * ROWS), :], n_r.at[0])
    wait(incoming.at[pl.ds(0, half_modes * NY - 1)], b_r.at[0])
    carried = [None] * MODES
    for p in range(half_modes):
        both = jnp.concatenate([incoming[p * NY + q] for q in range(NY)], axis=0)
        for m, late in (
            (p, jnp.where(even, both, next_down(both))),
            (p + half_modes, jnp.where(even, next_up(both), both)),
        ):
            carried[m] = jnp.where(even, seg_all[m] * late, late)

    def far_step(i, sums):
        t = SEG - 1 - i
        sums = tuple(dec_all[m] * s for m, s in enumerate(sums))
        acc = near[pl.ds(t, 8, stride=SEG), :]
        for m in range(MODES):
            acc = acc + resb_all[m] * sums[m]
        outf[pl.ds(t, 8, stride=SEG), :] = acc
        return sums

    lax.fori_loop(0, SEG, far_step, tuple(carried), unroll=UNROLL)
    for q in range(NY):
        out[:, q * LANES : (q + 1) * LANES] = outf[q * ROWS : (q + 1) * ROWS, :].astype(BF16)

    wait(rowsum_in.at[pl.ds(0, half_modes * NY - 1)], t_r.at[0])
    for m in range(MODES):
        for q in range(NY):
            j = m // half_modes
            rout[m : m + 1, q * LANES : (q + 1) * LANES] = rowsum_in[(m % half_modes) * NY + q, j : j + 1, :]

    wait(gobuf.at[pl.ds(0, 31)], go_s.at[0])
    wait(wbuf.at[pl.ds(0, 63)], z_s.at[0])
    wait(gtcv.at[pl.ds(0, 6)], gc_s.at[0])
    wait(arrived.at[pl.ds(0, NZ - 1)], a_s.at[0])
    wait(arrived.at[pl.ds(0, NZ - 1)], e_s.at[0])
    wait(inrow_in.at[pl.ds(0, NZ - 1)], i_s.at[0])
    wait(near.at[pl.ds(0, 3 * ROWS), :], n_s.at[0])
    wait(incoming.at[pl.ds(0, 31)], b_s.at[0])
    wait(incoming.at[pl.ds(0, 31)], t_s.at[0])


def local(grad_out, gate, conv_input, out_weight, residues, rates):
    hbm = pl.BlockSpec(memory_space=pltpu.HBM)
    vmem = pl.BlockSpec(memory_space=pltpu.VMEM)
    dma = pltpu.SemaphoreType.DMA

    def f32(*shape):
        return pltpu.VMEM(shape, F32)

    def bf16(*shape):
        return pltpu.VMEM(shape, BF16)

    operands = (grad_out, gate, conv_input, out_weight.T, residues, rates)
    operands = [pltpu.with_memory_space_constraint(a, pltpu.HBM) for a in operands]
    return pl.pallas_call(
        kernel,
        name="modal_backward",
        out_shape=(
            jax.ShapeDtypeStruct((ROWS, WIDE), BF16),
            jax.ShapeDtypeStruct((MODES, WIDE), F32),
        ),
        in_specs=[hbm] * 6,
        out_specs=(vmem, vmem),
        scratch_shapes=[
            bf16(2 * NX * NY, ROWS, WIDE),
            bf16(NY * NZ, 64, LANES),
            bf16(2 * NY, ROWS, LANES),
            f32(MODES, LANES),
            f32(MODES, LANES),
            f32(MODES, WIDE),
            f32(MODES, WIDE),
            f32(MODES, 8, LANES),
            f32(MODES, 8, LANES),
            f32(MODES, 8, LANES),
            f32(MODES, 8, LANES),
            f32(MODES, 8, LANES),
            f32(NY * ROWS, LANES),
            f32(NY * ROWS, LANES),
            f32(NY * ROWS, LANES),
            f32(NY * ROWS, LANES),
            f32(SEG, MODES, 8, LANES),
            f32(MODES, 8, LANES),
            f32(MODES // 2, 8, LANES),
            f32(NZ, 8, LANES),
            f32(MODES // 2, 8, LANES),
            f32(NZ, 8, LANES),
            f32(MODES // 2, 2, LANES),
            f32(NZ, 2, LANES),
            f32(MODES // 2 * NY, 2, LANES),
            f32(NZ, 8, LANES),
            f32(MODES // 2 * NY, 2, LANES),
            f32(2, LANES),
            f32(MODES // 2 * NY, 2, LANES),
            f32(NY * ROWS, LANES),
            dma((8,)),
            dma((1,)), dma((30,)), dma((1,)),
            dma((1,)), dma((24,)), dma((2,)), dma((4,)),
            dma((1,)), dma((1,)),
            dma((1,)), dma((1,)),
            dma((1,)), dma((1,)),
            dma((1,)), dma((1,)),
            dma((1,)), dma((1,)),
            dma((1,)), dma((1,)),
            dma((1,)), dma((1,)),
        ],
        compiler_params=pltpu.CompilerParams(
            collective_id=1, has_side_effects=True, vmem_limit_bytes=32 << 20
        ),
    )(*operands)


def solution(mesh):
    placed = (
        P("ctx", "tp"),
        P("ctx", "tp"),
        P("ctx", "tp"),
        P("tp", "ctx"),
        P(None, "tp"),
        P(None, "tp"),
    )
    return jax.shard_map(
        local,
        mesh=mesh,
        in_specs=placed,
        out_specs=(P("ctx", "tp"), P(None, "tp")),
        check_vma=False,
    )
```

```python
import jax
import jax.numpy as jnp
from jax import lax
from jax.experimental import pallas as pl
from jax.experimental.pallas import tpu as pltpu
from jax.sharding import PartitionSpec as P

MESH = pl.DeviceIdType.MESH
F32 = jnp.float32
BF16 = jnp.bfloat16
MODES = 16
NX = 4
NY = 4
NZ = 16
ROWS = 128
WIDE = 512
LANES = 128
SEG = 64
LENGTH = 8192
UNROLL = 4
HOPS = {0: (2, 1), 2: (2, 1), 4: (2, 1), 6: (2, 1)}


def kernel(
    go, gate, conv, weight, residues, rates,
    out, rout,
    gobuf, wbuf, gtcv, rt, rs, rt_all, rs_all,
    dec, resb, dec_all, resb_all, seg_all, gc, cvf, nearf, near, heads, ends, sent, arrived, sent_end, arrived_end,
    inrow, inrow_in, backs, late_all, incoming, rowsum, rowsum_in, outf,
    loc_sem, go_s, go_r, sib_r, z_s, z_r, leaf_r, y_r, gc_s, gc_r,
    a_s, a_r, e_s, e_r, i_s, i_r, n_s, n_r, b_s, b_r, t_s, t_r,
):
    ctx = lax.axis_index("ctx")
    tp = lax.axis_index("tp")
    x, k = tp // 2, tp % 2
    y, z = ctx // NZ, ctx % NZ
    xp, xm, x2 = (x + 1) % NX, (x + 3) % NX, (x + 2) % NX
    yp, ym, y2 = (y + 1) % NY, (y + 3) % NY, (y + 2) % NY

    def up(n):
        return (z + NZ + n) % NZ

    def dev(dx=None, dy=None, dz=None, dk=None):
        xx = x if dx is None else dx
        yy = y if dy is None else dy
        zz = z if dz is None else dz
        kk = k if dk is None else dk
        return (yy * NZ + zz, xx * 2 + kk)

    near_devices = [dev(dx=xp), dev(dx=xm), dev(dx=x2), dev(dk=1 - k)]
    near_devices += [dev(dz=up(n)) for n in (1, -1, 2, -2)]
    near_devices += [dev(dy=yy) for yy in (yp, ym, y2)]
    barrier = pltpu.get_barrier_semaphore()
    for d in near_devices:
        pl.semaphore_signal(barrier, inc=1, device_id=d, device_id_type=MESH)

    def send(src, dst, ss, rs_, target):
        pltpu.make_async_remote_copy(
            src_ref=src, dst_ref=dst, send_sem=ss, recv_sem=rs_, device_id=target, device_id_type=MESH
        ).start()

    def wait(ref, sem):
        pltpu.make_async_copy(ref, ref, sem).wait()

    def lanes(i):
        return pl.ds(pl.multiple_of(i * LANES, LANES), LANES)

    def shard(ox, core, oy):
        return (ox * 2 + core) * NY + oy

    def piece(r, owner):
        return r * NZ + owner

    cols = lanes(y)
    locals_ = [
        pltpu.make_async_copy(go, gobuf.at[shard(x, k, y)], loc_sem.at[0]),
        pltpu.make_async_copy(gate.at[:, cols], gtcv.at[y], loc_sem.at[1]),
        pltpu.make_async_copy(conv.at[:, cols], gtcv.at[NY + y], loc_sem.at[2]),
        pltpu.make_async_copy(rates.at[:, cols], rt, loc_sem.at[3]),
        pltpu.make_async_copy(residues.at[:, cols], rs, loc_sem.at[4]),
        pltpu.make_async_copy(weight.at[:, cols], wbuf.at[piece(0, z)], loc_sem.at[5]),
        pltpu.make_async_copy(rates, rt_all, loc_sem.at[6]),
        pltpu.make_async_copy(residues, rs_all, loc_sem.at[7]),
    ]
    for c in locals_:
        c.start()

    pl.semaphore_wait(barrier, len(near_devices))

    def z_slot(way, r, far):
        return (r * 2 + way) * 3 + far // 2 - 1

    def z_send(way, r, owner, far, hop, src=None, to=None):
        ref = wbuf.at[piece(r, owner)]
        target = dev(dy=to, dz=up(-hop if way else hop))
        if far in HOPS:
            sem = z_r.at[z_slot(way, r, far)]
        else:
            sem = leaf_r.at[0 if far < 6 else 1]
        send(ref if src is None else src, ref, z_s.at[0], sem, target)

    def z_wait(way, r, far):
        wait(wbuf.at[piece(r, up(far if way else -far))], z_r.at[z_slot(way, r, far)])

    for r in (0, 1, 3, 2):
        to = (y + NY - r) % NY
        src = weight.at[:, lanes(to)]
        for hop in HOPS[0] if r == 0 else ():
            for way in (0, 1):
                z_send(way, r, z, hop, hop, src, to)
    for r in (1, 3, 2):
        to = (y + NY - r) % NY
        send(weight.at[:, lanes(to)], wbuf.at[piece(r, z)], z_s.at[0], y_r.at[r], dev(dy=to))

    A, B = (0, 48), (48, 80)
    A0, A1, B0, B1 = (0, 32), (32, 16), (48, 48), (96, 32)
    go_slots = {}

    def go_ref(ox, oy, part):
        return gobuf.at[shard(ox, k, oy), pl.ds(part[0], part[1]), :]

    def go_send(key, ox, oy, part, target, src=None):
        slot = go_slots.setdefault(key, len(go_slots))
        ref = go_ref(ox, oy, part)
        send(ref if src is None else src, ref, go_s.at[0], go_r.at[slot], target)

    def go_wait(key, ox, oy, part):
        wait(go_ref(ox, oy, part), go_r.at[go_slots[key]])

    one_way = (("L", dev(dx=xp)), ("R", dev(dx=xm)), ("X2", dev(dx=x2)))
    other_way = (("D", dev(dy=yp)), ("U", dev(dy=ym)), ("Y2", dev(dy=y2)))
    for near_part, far_part in ((A, B), (B, A)):
        for way, part in ((one_way, near_part), (other_way, far_part)):
            for key, target in way:
                go_send((key, part), x, y, part, target, go.at[pl.ds(part[0], part[1]), :])

    sib_slots = []

    def sibling(ox, oy, src=None):
        ref = gobuf.at[shard(ox, k, oy)]
        send(ref if src is None else src, ref, go_s.at[0], sib_r.at[0], dev(dk=1 - k))
        sib_slots.append((ox, oy))

    sibling(x, y, go)

    def z_round(far, pieces=(0, 1, 3, 2)):
        for r in pieces:
            for way in (0, 1):
                owner = up(far if way else -far)
                z_wait(way, r, far)
                for hop in HOPS[far]:
                    if far + hop < 8 or way == r % 2:
                        z_send(way, r, owner, far + hop, hop)

    def y_pieces():
        for r in (1, 3, 2):
            wait(wbuf.at[piece(r, z)], y_r.at[r])
            for hop in HOPS[0]:
                for way in (0, 1):
                    z_send(way, r, z, hop, hop)

    columns = (("L", xm), ("R", xp), ("X2", x2))
    lines_ = (("D", ym), ("U", yp), ("Y2", y2))

    def turn(i):
        key, ox = columns[i]
        go_wait((key, A), ox, y, A)
        go_send((key, "D"), ox, y, A, dev(dy=yp))
        go_send((key, "U"), ox, y, A, dev(dy=ym))
        key, oy = lines_[i]
        go_wait((key, B), x, oy, B)
        go_send((key, "L"), x, oy, B, dev(dx=xp))
        go_send((key, "R"), x, oy, B, dev(dx=xm))

    def onward(i):
        key, ox = columns[i]
        go_wait((key, "D"), ox, ym, A)
        go_send((key, "Y2"), ox, ym, A0, dev(dy=yp))
        go_wait((key, "U"), ox, yp, A)
        go_send((key, "Y2"), ox, yp, A1, dev(dy=ym))
        key, oy = lines_[i]
        go_wait((key, "L"), xm, oy, B)
        go_send((key, "X2"), xm, oy, B0, dev(dx=xp))
        go_wait((key, "R"), xp, oy, B)
        go_send((key, "X2"), xp, oy, B1, dev(dx=xm))

    def gates():
        for r in range(1, NY):
            to = (y + r) % NY
            send(gate.at[:, lanes(to)], gtcv.at[y], gc_s.at[0], gc_r.at[0], dev(dy=to))
            send(conv.at[:, lanes(to)], gtcv.at[NY + y], gc_s.at[0], gc_r.at[0], dev(dy=to))

    def near_shards(i):
        key, ox = columns[i]
        go_wait((key, B), ox, y, B)
        sibling(ox, y)
        key, oy = lines_[i]
        go_wait((key, A), x, oy, A)
        sibling(x, oy)

    def diagonal_shards():
        for ox in (xm, xp):
            for oy in (ym, yp):
                sibling(ox, oy)

    def far_shards(i):
        key, ox = columns[i]
        go_wait((key, "Y2"), ox, y2, A)
        if i < 2:
            sibling(ox, y2)
        else:
            ref = go_ref(x2, y2, A)
            send(ref, ref, go_s.at[0], sib_r.at[0], dev(dk=1 - k))
        key, oy = lines_[i]
        go_wait((key, "X2"), x2, oy, B)
        if i < 2:
            sibling(x2, oy)
        else:
            ref = go_ref(x2, y2, B)
            send(ref, ref, go_s.at[0], sib_r.at[0], dev(dk=1 - k))

    def spread(ref, m):
        rows = [jnp.broadcast_to(ref[m : m + 1, q * LANES : (q + 1) * LANES], (2, LANES)) for q in range(NY)]
        return jnp.concatenate(rows, axis=0)

    def decays():
        for c in locals_:
            c.wait()
        for m in range(MODES):
            dec[m] = jnp.broadcast_to(jnp.exp(-rt[m : m + 1, :]), (8, LANES))
            resb[m] = jnp.broadcast_to(rs[m : m + 1, :], (8, LANES))
            rate = spread(rt_all, m)
            dec_all[m] = jnp.exp(-rate)
            seg_all[m] = jnp.exp(-rate * F32(SEG))
            resb_all[m] = spread(rs_all, m)

    row = lax.broadcasted_iota(jnp.int32, (8, LANES), 0)
    even = row % 2 == 0

    def by_seg(m):
        return jnp.broadcast_to(jnp.exp(-rt[m : m + 1, :] * F32(SEG)), (8, LANES))

    def next_up(v):
        return pltpu.roll(v, 7, 0)

    def next_down(v):
        return pltpu.roll(v, 1, 0)

    half_modes = MODES // 2
    far_first = [8]
    for d in range(7, 0, -1):
        far_first += [d, -d]

    zeros = tuple(jnp.zeros((8, LANES), F32) for _ in range(MODES))

    def head_step(t, sums):
        c = cvf[pl.ds(t, 8, stride=SEG), :]
        sums = tuple(dec[m] * s + c for m, s in enumerate(sums))
        for m, s in enumerate(sums):
            heads[t, m] = s
        return sums

    def input_ends():
        wait(gtcv.at[pl.ds(0, 6)], gc_r.at[0])
        cvf[...] = gtcv[NY : 2 * NY].reshape(NY * ROWS, LANES).astype(F32)
        sums = lax.fori_loop(0, SEG, head_step, zeros)
        sums = [dec[m] * s for m, s in enumerate(sums)]
        for m, s in enumerate(sums):
            ends[m] = s
        for p in range(half_modes):
            s, o = sums[p], sums[p + half_modes]
            sent_end[p] = jnp.where(even, next_up(s) + by_seg(p) * s, o + by_seg(p + half_modes) * next_down(o))
        arrived_end[z] = sent_end[z % half_modes]

    def send_ends(chips):
        for d in chips:
            send(sent_end.at[up(d) % half_modes], arrived_end.at[z], e_s.at[0], e_r.at[0], dev(dz=up(d)))

    def z_leaves(group):
        wait(wbuf.at[pl.ds(0, 24 if group == 0 else 12)], leaf_r.at[group])

    y_pieces()
    z_round(2, (0,))
    turn(0)
    turn(1)
    z_round(2, (1, 3, 2))
    turn(2)
    decays()
    near_shards(0)
    near_shards(1)
    near_shards(2)
    gates()
    z_round(4, (0, 1))
    onward(0)
    z_round(4, (3, 2))
    onward(1)
    diagonal_shards()
    onward(2)
    z_round(6, (0, 1))
    input_ends()
    far_shards(0)
    z_round(6, (3, 2))
    z_leaves(0)
    send_ends((6, -6, 5, -5, 4, -4, 3, -3, 2, -2, 1, -1))
    far_shards(1)
    far_shards(2)
    z_leaves(1)
    send_ends((8, 7, -7))
    wait(gobuf.at[pl.ds(0, NX * NY)], sib_r.at[0])

    total = jnp.zeros((NY * ROWS, LANES), F32)
    for ox in range(NX):
        rel = (ox + NY - y) % NY
        for half in range(2):
            a = gobuf[(ox * 2 + half) * NY : (ox * 2 + half + 1) * NY].reshape(NY * ROWS, WIDE)
            w = wbuf[pl.ds(rel * NZ + half * 8, 8)].reshape(WIDE, LANES)
            total = total + jnp.dot(a, w, preferred_element_type=F32)
    gc[...] = total * gtcv[:NY].reshape(NY * ROWS, LANES).astype(F32)

    def start_step(i, sums):
        g = gc[pl.ds(SEG - 1 - i, 8, stride=SEG), :]
        return tuple(dec[m] * s + g for m, s in enumerate(sums))

    sums = lax.fori_loop(0, SEG, start_step, zeros, unroll=UNROLL)
    for p in range(half_modes):
        s, o = sums[p], sums[p + half_modes]
        sent[p] = jnp.where(even, s + by_seg(p) * next_up(s), next_down(o) + by_seg(p + half_modes) * o)

    arrived[z] = sent[z % half_modes]
    for d in far_first:
        send(sent.at[up(d) % half_modes], arrived.at[z], a_s.at[0], a_r.at[0], dev(dz=up(d)))
    def inner_step(t, inner):
        g = gc[pl.ds(t, 8, stride=SEG), :]
        return tuple(n + g * heads[t, m] for m, n in enumerate(inner))

    inner = lax.fori_loop(0, SEG, inner_step, zeros, unroll=UNROLL)
    from_second = tuple(jnp.where(even, next_up(s), 0.0) for s in sums)
    inner = [n + ends[m] * s for m, (n, s) in enumerate(zip(inner, from_second))]
    for m in range(MODES):
        inrow[m % half_modes, m // half_modes : m // half_modes + 1, :] = jnp.sum(inner[m], axis=0, keepdims=True)
    inrow_in[z] = inrow[z % half_modes]
    for d in far_first:
        send(inrow.at[up(d) % half_modes], inrow_in.at[z], i_s.at[0], i_r.at[0], dev(dz=up(d)))

    def near_step(i, sums):
        t = SEG - 1 - i
        g = gc[pl.ds(t, 8, stride=SEG), :]
        sums = tuple(dec[m] * s + g for m, s in enumerate(sums))
        acc = resb[0] * sums[0]
        for m in range(1, MODES):
            acc = acc + resb[m] * sums[m]
        nearf[pl.ds(t, 8, stride=SEG), :] = acc
        return sums

    lax.fori_loop(0, SEG, near_step, from_second, unroll=UNROLL)
    for r in (2, 1, 3):
        to = (y + r) % NY
        rows = pl.ds(pl.multiple_of(to * ROWS, ROWS), ROWS)
        mine = pl.ds(pl.multiple_of(y * ROWS, ROWS), ROWS)
        send(nearf.at[rows, :], near.at[mine, :], n_s.at[0], n_r.at[0], dev(dy=to))
    near[mine, :] = nearf[mine, :]

    pair = z % half_modes
    rate = jnp.where(even, rt[pl.ds(pair, 1), :], rt[pl.ds(pair + half_modes, 1), :])
    by_block = jnp.exp(-rate * F32(ROWS))
    by_line = jnp.exp(-rate * F32(ROWS * NZ))
    to_line = [jnp.exp(-rate * F32(ROWS * (NZ - 1 - zz))) for zz in range(NZ)]
    wait(arrived.at[pl.ds(0, NZ - 1)], a_r.at[0])
    after = [None] * NZ
    after[NZ - 1] = jnp.zeros((8, LANES), F32)
    for zz in range(NZ - 2, -1, -1):
        after[zz] = arrived[zz + 1] + by_block * after[zz + 1]
    line = arrived[0] + by_block * after[0]

    def next_line(v):
        return jnp.where(row < 6, pltpu.roll(v, 6, 0), 0.0)

    line_next = next_line(line)
    lines = line_next
    for _ in range(NY - 2):
        lines = line_next + by_line * next_line(lines)
    ins = []
    for zz in range(NZ):
        ins.append(after[zz] + to_line[zz] * lines)
        late_all[zz] = ins[zz]

    served = (-4, 3, -3, 2, -2, 1, -1, 0)
    slot = pair * NY + y
    for i, d in enumerate(served):
        late = late_all[up(d)]
        for b in range(NY):
            backs[i * NY + b] = late[2 * b : 2 * b + 2]
        if d == 0:
            incoming[slot] = backs[i * NY + y]
        for r in (2, 1, 3, 0):
            if d or r:
                to = (y + r) % NY
                send(backs.at[i * NY + to], incoming.at[slot], b_s.at[0], b_r.at[0], dev(dy=to, dz=up(d)))

    wait(arrived_end.at[pl.ds(0, NZ - 1)], e_r.at[0])
    grad = jnp.zeros((8, LANES), F32)
    for zz in range(NZ):
        grad = grad + arrived_end[zz] * ins[zz]
    grad = grad + pltpu.roll(grad, 4, 0)
    grad = (grad + pltpu.roll(grad, 2, 0))[:2]
    wait(inrow_in.at[pl.ds(0, NZ - 1)], i_r.at[0])
    for zz in range(NZ):
        grad = grad + inrow_in[zz]
    rowsum[...] = grad * F32(1.0 / LENGTH)
    rowsum_in[slot] = rowsum[...]
    for d in served:
        for r in (2, 1, 3, 0):
            if d or r:
                to = (y + r) % NY
                send(rowsum, rowsum_in.at[slot], t_s.at[0], t_r.at[0], dev(dy=to, dz=up(d)))

    wait(near.at[pl.ds(0, 3 * ROWS), :], n_r.at[0])
    wait(incoming.at[pl.ds(0, half_modes * NY - 1)], b_r.at[0])
    carried = [None] * MODES
    for p in range(half_modes):
        both = jnp.concatenate([incoming[p * NY + q] for q in range(NY)], axis=0)
        for m, late in (
            (p, jnp.where(even, both, next_down(both))),
            (p + half_modes, jnp.where(even, next_up(both), both)),
        ):
            carried[m] = jnp.where(even, seg_all[m] * late, late)

    def far_step(i, sums):
        t = SEG - 1 - i
        sums = tuple(dec_all[m] * s for m, s in enumerate(sums))
        acc = near[pl.ds(t, 8, stride=SEG), :]
        for m in range(MODES):
            acc = acc + resb_all[m] * sums[m]
        outf[pl.ds(t, 8, stride=SEG), :] = acc
        return sums

    lax.fori_loop(0, SEG, far_step, tuple(carried), unroll=UNROLL)
    for q in range(NY):
        out[:, q * LANES : (q + 1) * LANES] = outf[q * ROWS : (q + 1) * ROWS, :].astype(BF16)

    wait(rowsum_in.at[pl.ds(0, half_modes * NY - 1)], t_r.at[0])
    for m in range(MODES):
        for q in range(NY):
            j = m // half_modes
            rout[m : m + 1, q * LANES : (q + 1) * LANES] = rowsum_in[(m % half_modes) * NY + q, j : j + 1, :]

    wait(gobuf.at[pl.ds(0, 31)], go_s.at[0])
    wait(wbuf.at[pl.ds(0, 63)], z_s.at[0])
    wait(gtcv.at[pl.ds(0, 6)], gc_s.at[0])
    wait(arrived.at[pl.ds(0, NZ - 1)], a_s.at[0])
    wait(arrived.at[pl.ds(0, NZ - 1)], e_s.at[0])
    wait(inrow_in.at[pl.ds(0, NZ - 1)], i_s.at[0])
    wait(near.at[pl.ds(0, 3 * ROWS), :], n_s.at[0])
    wait(incoming.at[pl.ds(0, 31)], b_s.at[0])
    wait(incoming.at[pl.ds(0, 31)], t_s.at[0])


def local(grad_out, gate, conv_input, out_weight, residues, rates):
    hbm = pl.BlockSpec(memory_space=pltpu.HBM)
    vmem = pl.BlockSpec(memory_space=pltpu.VMEM)
    dma = pltpu.SemaphoreType.DMA

    def f32(*shape):
        return pltpu.VMEM(shape, F32)

    def bf16(*shape):
        return pltpu.VMEM(shape, BF16)

    operands = (grad_out, gate, conv_input, out_weight.T, residues, rates)
    operands = [pltpu.with_memory_space_constraint(a, pltpu.HBM) for a in operands]
    return pl.pallas_call(
        kernel,
        name="modal_backward",
        out_shape=(
            jax.ShapeDtypeStruct((ROWS, WIDE), BF16),
            jax.ShapeDtypeStruct((MODES, WIDE), F32),
        ),
        in_specs=[hbm] * 6,
        out_specs=(vmem, vmem),
        scratch_shapes=[
            bf16(2 * NX * NY, ROWS, WIDE),
            bf16(NY * NZ, 64, LANES),
            bf16(2 * NY, ROWS, LANES),
            f32(MODES, LANES),
            f32(MODES, LANES),
            f32(MODES, WIDE),
            f32(MODES, WIDE),
            f32(MODES, 8, LANES),
            f32(MODES, 8, LANES),
            f32(MODES, 8, LANES),
            f32(MODES, 8, LANES),
            f32(MODES, 8, LANES),
            f32(NY * ROWS, LANES),
            f32(NY * ROWS, LANES),
            f32(NY * ROWS, LANES),
            f32(NY * ROWS, LANES),
            f32(SEG, MODES, 8, LANES),
            f32(MODES, 8, LANES),
            f32(MODES // 2, 8, LANES),
            f32(NZ, 8, LANES),
            f32(MODES // 2, 8, LANES),
            f32(NZ, 8, LANES),
            f32(MODES // 2, 2, LANES),
            f32(NZ, 2, LANES),
            f32(MODES // 2 * NY, 2, LANES),
            f32(NZ, 8, LANES),
            f32(MODES // 2 * NY, 2, LANES),
            f32(2, LANES),
            f32(MODES // 2 * NY, 2, LANES),
            f32(NY * ROWS, LANES),
            dma((8,)),
            dma((1,)), dma((30,)), dma((1,)),
            dma((1,)), dma((24,)), dma((2,)), dma((4,)),
            dma((1,)), dma((1,)),
            dma((1,)), dma((1,)),
            dma((1,)), dma((1,)),
            dma((1,)), dma((1,)),
            dma((1,)), dma((1,)),
            dma((1,)), dma((1,)),
            dma((1,)), dma((1,)),
        ],
        compiler_params=pltpu.CompilerParams(
            collective_id=1, has_side_effects=True, vmem_limit_bytes=32 << 20
        ),
    )(*operands)


def solution(mesh):
    placed = (
        P("ctx", "tp"),
        P("ctx", "tp"),
        P("ctx", "tp"),
        P("tp", "ctx"),
        P(None, "tp"),
        P(None, "tp"),
    )
    return jax.shard_map(
        local,
        mesh=mesh,
        in_specs=placed,
        out_specs=(P("ctx", "tp"), P(None, "tp")),
        check_vma=False,
    )
```
